256 devices in a mesh: rep: 16 (over y, z_lo), tp: 16 (over z_hi, x, core).
Axes of the slice: x: 4, y: 4, z: 8 (z_hi: 2, z_lo: 4; z = z_hi * 4 + z_lo), core: 2. Of those that a mesh axis runs over, the one named last changes fastest.
Arguments:
- hidden_act: bfloat16 [16, 2048, 28672], P('rep', None, 'tp'), may hold values from -6 to 6
- out_grads: bfloat16 [16, 2048, 384], P('rep', 'tp'), may hold values from -0.125 to 0.125
- momentum: float32 [16, 28672, 384], P('rep', 'tp'), may hold values from -6 to 6
- coeff_index: int32 [16, 448, 6, 32], P(None, 'tp'), may hold values from 0 to 4095, as said below
Outputs:
- new_momentum: float32 [16, 28672, 384], P('rep', 'tp')
- update: bfloat16 [28672, 384], P('tp')
The draws below stay inside these ranges and needn't reach their ends.
Inputs may be any that keep to these rules, and one draw needn't show every extreme that they name: `coeff_index`: the 32 indices of one block of one replica are distinct.
All inputs are finite; a program needn't handle non-finite values.
Results may differ from the reference program's by a relative error of at most 0.001.
Values may be sent and summed in bfloat16 or wider, within the bound.
A program may use at most 128 MiB of HBM per device.

```python
import jax
import jax.numpy as jnp
from jax import lax

FF = 28672
COLS = 384
TOK = 2048
SPAN = 64
TOPK = 32
N_REP = 16


def draw_coeff_index(key, part):
    key = jax.random.fold_in(key, 7)
    shape = (N_REP, FF // SPAN, COLS // SPAN, SPAN * SPAN)
    scores = jax.random.randint(key, shape, 0, 2 ** 18) * (SPAN * SPAN) + jnp.arange(SPAN * SPAN)
    return jax.lax.top_k(scores, TOPK)[1].astype(jnp.int32)


def shard_levels(key, extent, shards, least, largest):
    factor_of, own = 1.0, jax.random.fold_in(key, 6)
    for dim, blocks in shards:
        heights = jnp.exp(jax.random.uniform(jax.random.fold_in(own, dim), (blocks,), jnp.float32, least / len(shards), largest / len(shards)))
        factor_of = factor_of * jnp.repeat(heights, extent[dim] // blocks).reshape([-1 if axis == dim else 1 for axis in range(len(extent))])
    return factor_of


def noise(key, extent, spread, reach, split=(), held_as=jnp.bfloat16):
    values = spread * jax.random.normal(key, extent, jnp.float32)
    if split:
        values = values * shard_levels(key, extent, split, -0.22, 0.18)
    return jnp.clip(values, -reach, reach).astype(held_as)


def setup_inputs(seed: int = 0) -> dict:
    seeds = jax.random.split(jax.random.key(seed), 5)
    hidden_act = noise(seeds[0], (N_REP, TOK, FF), 1.0, 6.0, ((0, 16), (2, 16)))
    out_grads = noise(seeds[1], (N_REP, TOK, COLS), TOK ** -0.5, 0.125, ((0, 16), (1, 16)))
    momentum = noise(seeds[2], (N_REP, FF, COLS), 1.0, 6.0, ((0, 16), (1, 16)), jnp.float32)
    coeff_index = draw_coeff_index(jax.random.fold_in(seeds[4], 71), 0)
    return dict(hidden_act=hidden_act, out_grads=out_grads, momentum=momentum, coeff_index=coeff_index)


decay_rate = 0.9

def dct_table():
    pos = jnp.arange(SPAN).astype(jnp.float32)
    freq = jnp.arange(SPAN).astype(jnp.float32)[:, None]
    scale = jnp.where(freq == 0.0, jnp.sqrt(1.0 / SPAN), jnp.sqrt(2.0 / SPAN)).astype(jnp.float32)
    return (scale * jnp.cos(jnp.pi * (2.0 * pos[None, :] + 1.0) * freq / (2.0 * SPAN))).astype(jnp.float32)

def forward_blocks(field, table):
    blocks = field.reshape(FF // SPAN, SPAN, COLS // SPAN, SPAN)
    half = jnp.einsum('un,anbm->aubm', table, blocks, precision=lax.Precision.HIGHEST)
    return jnp.einsum('aubm,vm->aubv', half, table, precision=lax.Precision.HIGHEST)

def inverse_blocks(spectra, table):
    half = jnp.einsum('un,aubv->anbv', table, spectra, precision=lax.Precision.HIGHEST)
    full = jnp.einsum('anbv,vm->anbm', half, table, precision=lax.Precision.HIGHEST)
    return full.reshape(FF, COLS)

def reference(hidden_act, out_grads, momentum, coeff_index):
    table = dct_table()
    rows_a = jnp.arange(FF // SPAN)[:, None, None]
    rows_b = jnp.arange(COLS // SPAN)[None, :, None]

    def one_replica(items):
        acts, grads, moment, index = items
        grad = jnp.dot(acts.T, grads, preferred_element_type=jnp.float32)
        mixed = decay_rate * moment + grad
        spectrum = forward_blocks(mixed, table)
        values = spectrum[rows_a, index // SPAN, rows_b, index % SPAN]
        sparse = jnp.zeros(spectrum.shape, jnp.float32).at[rows_a, index // SPAN, rows_b, index % SPAN].add(values)
        kept = inverse_blocks(sparse, table)
        return (mixed - kept, values)
    new_momentum, values = lax.map(one_replica, (hidden_act, out_grads, momentum, coeff_index))
    total = jnp.zeros((FF // SPAN, SPAN, COLS // SPAN, SPAN), jnp.float32)
    total = total.at[rows_a[None], coeff_index // SPAN, rows_b[None], coeff_index % SPAN].add(values)
    decoded = inverse_blocks(total, table).reshape(FF // SPAN, SPAN, COLS // SPAN, SPAN)
    meansq = lax.optimization_barrier(jnp.mean(decoded * decoded, axis=(1, 3), keepdims=True))
    update = jnp.tanh(decoded / jnp.sqrt(meansq + 1e-06)).reshape(FF, COLS).astype(jnp.bfloat16)
    return (new_momentum, update)
```

```python
import functools

import jax
import jax.numpy as jnp
import ml_dtypes
import numpy as np
from jax import lax
from jax.experimental import pallas as pl
from jax.experimental.pallas import tpu as pltpu
from jax.sharding import PartitionSpec as P

SPAN = 64
DECAY = 0.9
MESH = pl.DeviceIdType.MESH
f32, bf16, i32 = jnp.float32, jnp.bfloat16, jnp.int32


def dct_table():
    n = np.arange(SPAN)
    u = np.arange(SPAN)[:, None]
    scale = np.where(u == 0, np.sqrt(1.0 / SPAN), np.sqrt(2.0 / SPAN))
    return (scale * np.cos(np.pi * (2 * n[None] + 1) * u / (2 * SPAN))).astype(np.float32)


def split_table(x):
    high = x.astype(ml_dtypes.bfloat16)
    low = (x - high.astype(np.float32)).astype(ml_dtypes.bfloat16)
    return high, low


def split(x):
    high = x.astype(bf16)
    return high, (x - high.astype(f32)).astype(bf16)


def dot(a, b):
    return jnp.dot(a, b, preferred_element_type=f32)


def dot_t(a, b):
    return lax.dot_general(a, b, (((1,), (1,)), ((), ())), preferred_element_type=f32)


def dot3(ah, al, bh, bl):
    return dot(ah, bh) + dot(al, bh) + dot(ah, bl)


def lane_gather(x, idx):
    return jnp.take_along_axis(x, idx, axis=1, mode="promise_in_bounds")


def exchange_kernel(
    og_hbm, act_hbm, mom_hbm, idx_hbm, dth, dtl, ct2,
    newmom_hbm, vals, iu, iv,
    act, og, gt, mixed, idx, cu, rh, rl, wrow,
    load_sem, og_send, og_recv, v_send, v_recv, out_sem,
):
    rep, tp = lax.axis_index("rep"), lax.axis_index("tp")
    y, zl = rep // 4, rep % 4
    zh, x, c = tp // 8, (tp // 2) % 4, tp % 2
    tok = og_hbm.shape[1]

    def tpid(zh_, x_, c_):
        return (zh_ * 4 + x_) * 2 + c_

    xs = [lax.rem(x + 1, 4), lax.rem(x + 3, 4), lax.rem(x + 2, 4)]
    x_peers = [tpid(zh, xx, c) for xx in xs]
    core_peer = tpid(zh, x, 1 - c)
    z_peer = tpid(1 - zh, x, c)
    z_reps = [y * 4 + lax.rem(zl + d, 4) for d in (1, 2, 3)]
    y_reps = [lax.rem(y + d, 4) * 4 + zl for d in (1, 3, 2)]

    loads = []

    def load(src, dst):
        cp = pltpu.make_async_copy(src, dst, load_sem.at[len(loads)])
        cp.start()
        loads.append(cp)
        return cp

    def slot(t):
        return pl.ds(pl.multiple_of(t * tok, tok), tok)

    og_in = load(og_hbm.at[0], og.at[slot(tp)])
    idx_in = load(idx_hbm, idx)
    half = 4 * 2 * tok
    act_in = []
    for h in (zh, 1 - zh):
        rows = pl.ds(pl.multiple_of(h * half, half), half)
        act_in.append(load(act_hbm.at[0, rows], act.at[rows]))
    mom_in = load(mom_hbm.at[0], mixed)

    barrier = pltpu.get_barrier_semaphore()
    for t in x_peers + [core_peer, z_peer]:
        pl.semaphore_signal(barrier, inc=1, device_id=(rep, t), device_id_type=MESH)
    for r in z_reps + y_reps:
        pl.semaphore_signal(barrier, inc=1, device_id=(r, tp), device_id_type=MESH)
    pl.semaphore_wait(barrier, 11)

    sends = []

    def send(src_tp, dst_tp):
        cp = pltpu.make_async_remote_copy(
            src_ref=og.at[slot(src_tp)],
            dst_ref=og.at[slot(src_tp)],
            send_sem=og_send.at[len(sends)],
            recv_sem=og_recv.at[src_tp],
            device_id=(rep, dst_tp),
            device_id_type=MESH,
        )
        cp.start()
        sends.append(cp)

    def arrived(src_tp):
        pltpu.make_async_remote_copy(
            src_ref=og.at[slot(src_tp)],
            dst_ref=og.at[slot(src_tp)],
            send_sem=og_send.at[0],
            recv_sem=og_recv.at[src_tp],
            device_id=(rep, tp),
            device_id_type=MESH,
        ).wait_recv()

    og_in.wait()
    send(tp, z_peer)
    for t in x_peers:
        send(tp, t)
    send(tp, core_peer)

    idx_in.wait()

    def index_rows(a, _):
        for g in range(4):
            row = jnp.concatenate([idx[4 * g + i, a] for i in range(4)], axis=1)
            iu[a, g, 0:6, :] = (row >> 6).astype(f32)
            iv[a, g, 0:6, :] = (row & 63).astype(f32)
        return 0

    lax.fori_loop(0, 28, index_rows, 0)

    def own_tables(j, _):
        row_b = lax.broadcasted_iota(i32, (128, 128), 0) // 64
        lane = lax.broadcasted_iota(i32, (128, 128), 1)
        mine = row_b == (lane // 32) % 2
        for q in range(6):
            a2, bp = q // 3, q % 3
            row = jnp.concatenate(
                [idx[rep, 4 * j + 2 * a2 + ap, 2 * bp + b : 2 * bp + b + 1, :] for ap in range(2) for b in range(2)],
                axis=1,
            )
            k = j * 6 + q
            cu[k] = lane_gather(ct2[...], jnp.broadcast_to(row >> 6, (64, 128)))
            cv = lane_gather(ct2[...], jnp.broadcast_to(row & 63, (64, 128)))
            cvh, cvl = split(jnp.where(mine, jnp.concatenate([cv, cv], axis=0), 0.0))
            rh[k] = cvh
            rl[k] = cvl
        return 0

    lax.fori_loop(0, 7, own_tables, 0)

    for t in x_peers:
        arrived(t)
        send(t, core_peer)
    arrived(z_peer)
    for t in x_peers:
        send(z_peer, t)
    send(z_peer, core_peer)

    arrived(core_peer)
    for xx in xs:
        arrived(tpid(zh, xx, 1 - c))
    act_in[0].wait()

    def partial_grad(off, depth, first):
        off = pl.multiple_of(off, depth)
        bt = og[pl.ds(off, depth), :].T

        def body(j, _):
            cols = pl.ds(pl.multiple_of(j * 256, 256), 256)
            part = dot(bt, act[pl.ds(off, depth), cols])
            gt[:, cols] = part if first else gt[:, cols] + part
            return 0

        lax.fori_loop(0, 7, body, 0)

    partial_grad(zh * half, half, True)

    for xx in xs:
        t = tpid(1 - zh, xx, c)
        arrived(t)
        send(t, core_peer)
    act_in[1].wait()
    mom_in.wait()
    arrived(tpid(1 - zh, x, 1 - c))
    for xx in xs:
        arrived(tpid(1 - zh, xx, 1 - c))

    off2 = pl.multiple_of((1 - zh) * half, half)
    bt2 = og[pl.ds(off2, half), :].T

    def forward(j, _):
        cols = pl.ds(pl.multiple_of(j * 256, 256), 256)
        g = gt[:, cols] + dot(bt2, act[pl.ds(off2, half), cols])
        m = DECAY * mixed[cols, :] + g.T
        mixed[cols, :] = m
        mh, ml = split(m)
        lane = lax.broadcasted_iota(i32, (64, 128), 1)
        ws = []
        hs = [dot3(mh[:, :256], ml[:, :256], dth[...], dtl[...])]
        hs.append(dot3(mh[:, 256:], ml[:, 256:], dth[:128, :128], dtl[:128, :128]))
        hs = [hs[0][:, :128], hs[0][:, 128:], hs[1]]
        for q in range(6):
            a2, bp = q // 3, q % 3
            row = jnp.concatenate(
                [
                    (idx[rep, 4 * j + 2 * a2 + ap, 2 * bp + b : 2 * bp + b + 1, :] & 63) + 64 * b
                    for ap in range(2)
                    for b in range(2)
                ],
                axis=1,
            )
            ib = jnp.broadcast_to(row, (64, 128))
            h = hs[bp][128 * a2 : 128 * a2 + 128]
            got = jnp.where(lane < 64, lane_gather(h[:64], ib), lane_gather(h[64:], ib))
            w = jnp.sum(got * cu[j * 6 + q], axis=0, keepdims=True)
            wrow[pl.ds(j * 6 + q, 1), :] = w
            ws.append(w)
        rows = []
        for b in range(6):
            bp, bo = b // 2, 32 * (b % 2)
            rows.append(
                jnp.concatenate([ws[3 * a2 + bp][:, o + bo : o + bo + 32] for a2 in range(2) for o in (0, 64)], axis=1)
            )
        vals[rep, j] = jnp.concatenate(rows + [jnp.zeros((2, 128), f32)], axis=0)
        return 0

    def vcopy(r, to, lo, n, si, ri):
        return pltpu.make_async_remote_copy(
            src_ref=vals.at[r, pl.ds(lo, n)],
            dst_ref=vals.at[r, pl.ds(lo, n)],
            send_sem=v_send.at[si],
            recv_sem=v_recv.at[r, ri],
            device_id=(to, tp),
            device_id_type=MESH,
        )

    groups = [(0, 4), (4, 3)]
    vsends = []

    def vsend(r, to, gi):
        cp = vcopy(r, to, *groups[gi], len(vsends), gi)
        cp.start()
        vsends.append(cp)

    def varrived(r, gi):
        vcopy(r, rep, *groups[gi], 0, gi).wait_recv()

    lax.fori_loop(0, 4, forward, 0)
    for r in z_reps + y_reps:
        vsend(rep, r, 0)
    lax.fori_loop(4, 7, forward, 0)
    for r in z_reps + y_reps:
        vsend(rep, r, 1)
    for z in z_reps:
        varrived(z, 0)
        for r in y_reps:
            vsend(z, r, 0)

    outs = []

    def keep(j, _):
        lane = lax.broadcasted_iota(i32, (64, 128), 1)
        for q in range(6):
            a2, bp = q // 3, q % 3
            k = j * 6 + q
            l = cu[k] * jnp.broadcast_to(wrow[pl.ds(k, 1), :], (64, 128))
            lh, ll = split(jnp.concatenate([jnp.where(lane < 64, l, 0.0), jnp.where(lane < 64, 0.0, l)], axis=0))
            kept = dot_t(lh, rh[k]) + dot_t(ll, rh[k]) + dot_t(lh, rl[k])
            rows = pl.ds(pl.multiple_of(j * 256 + a2 * 128, 128), 128)
            cols = slice(bp * 128, bp * 128 + 128)
            mixed[rows, cols] = mixed[rows, cols] - kept
        return 0

    def write(lo, n):
        rows = pl.ds(lo * 256, n * 256)
        cp = pltpu.make_async_copy(mixed.at[rows], newmom_hbm.at[rows], out_sem.at[len(outs)])
        cp.start()
        outs.append(cp)

    lax.fori_loop(0, 4, keep, 0)
    write(0, 4)
    for z in z_reps:
        varrived(z, 1)
        for r in y_reps:
            vsend(z, r, 1)
    lax.fori_loop(4, 7, keep, 0)
    write(4, 3)

    for yr in y_reps:
        for gi in range(2):
            varrived(yr, gi)
        for d in (1, 2, 3):
            for gi in range(2):
                varrived((yr // 4) * 4 + lax.rem(zl + d, 4), gi)
    for cp in sends + vsends:
        cp.wait_send()
    for cp in outs:
        cp.wait()


def exchange(og, act, mom, idx):
    rows, cols = mom.shape[1:]
    tok = act.shape[1]
    table = dct_table()
    dth, dtl = split_table(np.kron(np.eye(4, dtype=np.float32), table.T))
    ct2 = np.concatenate([table.T, table.T], axis=1)
    vmem = pl.BlockSpec(memory_space=pltpu.VMEM)
    anyw = pl.BlockSpec(memory_space=pl.ANY)
    S = jax.ShapeDtypeStruct
    return pl.pallas_call(
        exchange_kernel,
        out_shape=(
            S((rows, cols), f32),
            S((16, 7, 8, 128), f32),
            S((28, 4, 8, 128), f32),
            S((28, 4, 8, 128), f32),
        ),
        in_specs=[anyw] * 4 + [vmem] * 3,
        out_specs=(anyw, vmem, vmem, vmem),
        scratch_shapes=[
            pltpu.VMEM((tok, rows), bf16),
            pltpu.VMEM((tok, cols), bf16),
            pltpu.VMEM((cols, rows), f32),
            pltpu.VMEM((rows, cols), f32),
            pltpu.VMEM(idx.shape, i32),
            pltpu.VMEM((42, 64, 128), f32),
            pltpu.VMEM((42, 128, 128), bf16),
            pltpu.VMEM((42, 128, 128), bf16),
            pltpu.VMEM((48, 128), f32),
            pltpu.SemaphoreType.DMA((5,)),
            pltpu.SemaphoreType.DMA((16,)),
            pltpu.SemaphoreType.DMA((16,)),
            pltpu.SemaphoreType.DMA((32,)),
            pltpu.SemaphoreType.DMA((16, 2)),
            pltpu.SemaphoreType.DMA((2,)),
        ],
        compiler_params=pltpu.CompilerParams(collective_id=0, has_side_effects=True, vmem_limit_bytes=56 << 20),
        name="exchange",
    )(og, act, mom, idx, dth, dtl, ct2)


def decode_kernel(
    newmom_in, vals, iu, iv, dth, dtl, dch, dcl, newmom, update, s_buf, v_buf, sem
):
    cp = pltpu.make_async_copy(newmom_in, newmom.at[0], sem)
    cp.start()
    io = lax.broadcasted_iota(i32, (64, 128), 0).astype(f32).astype(bf16)
    io2 = lax.broadcasted_iota(i32, (128, 128), 0).astype(f32).astype(bf16)
    zero, zero2 = jnp.zeros((64, 128), bf16), jnp.zeros((128, 128), bf16)
    one2 = jnp.ones((128, 128), bf16)

    def spread(row, n):
        return jnp.broadcast_to(row, (n, 128)).astype(bf16)

    def body(j, _):
        for g in range(4):
            got = [vals[4 * g + i, j] for i in range(4)]
            for ai in range(4):
                v_buf[ai, g] = jnp.concatenate([v[:, 32 * ai : 32 * ai + 32] for v in got], axis=1)
        for ai in range(4):
            for bp in range(3):
                left, right = [], []
                for bo in range(2):
                    b = 2 * bp + bo
                    for g in range(4):
                        hit = spread(iu[4 * j + ai, g, b : b + 1, :], 64) == io
                        v = v_buf[ai, g, b : b + 1, :]
                        vh = v.astype(bf16).astype(f32)
                        left.append(
                            jnp.concatenate(
                                [jnp.where(hit, spread(vh, 64), zero), jnp.where(hit, spread(v - vh, 64), zero)], axis=0
                            )
                        )
                        at = spread(iv[4 * j + ai, g, b : b + 1, :] + 64.0 * bo, 128)
                        right.append(jnp.where(at == io2, one2, zero2))
                o = dot_t(jnp.concatenate(left, axis=1), jnp.concatenate(right, axis=1))
                s_buf[64 * ai : 64 * ai + 64, 128 * bp : 128 * bp + 128] = o[:64] + o[64:]
        sh, sl = split(s_buf[...])
        t = jnp.concatenate(
            [
                dot3(sh[:, :256], sl[:, :256], dch[...], dcl[...]),
                dot3(sh[:, 256:], sl[:, 256:], dch[:128, :128], dcl[:128, :128]),
            ],
            axis=1,
        )
        th, tl = split(t)
        d = dot3(dth[...], dtl[...], th, tl)
        lane = lax.broadcasted_iota(i32, (1, 128), 1)
        for ai in range(4):
            for bp in range(3):
                blk = d[64 * ai : 64 * ai + 64, 128 * bp : 128 * bp + 128]
                col = jnp.sum(blk * blk, axis=0, keepdims=True)
                lo = jnp.sum(jnp.where(lane < 64, col, 0.0), axis=1, keepdims=True)
                hi = jnp.sum(jnp.where(lane < 64, 0.0, col), axis=1, keepdims=True)
                q = jnp.where(lane < 64, lo, hi) * (1.0 / (SPAN * SPAN))
                update[pl.ds(pl.multiple_of(j * 256 + 64 * ai, 64), 64), 128 * bp : 128 * bp + 128] = jnp.tanh(
                    blk * lax.rsqrt(q + 1e-06)
                ).astype(bf16)
        return 0

    lax.fori_loop(0, 7, body, 0)
    cp.wait()


def decode(newmom, vals, iu, iv):
    rows, cols = newmom.shape
    table = dct_table()
    dt = np.kron(np.eye(4, dtype=np.float32), table.T)
    dth, dtl = split_table(dt)
    dch, dcl = split_table(dt.T.copy())
    vmem = pl.BlockSpec(memory_space=pltpu.VMEM)
    anyw = pl.BlockSpec(memory_space=pl.ANY)
    S = jax.ShapeDtypeStruct
    return pl.pallas_call(
        decode_kernel,
        out_shape=(S((1, rows, cols), f32), S((rows, cols), bf16)),
        in_specs=[anyw] + [vmem] * 7,
        out_specs=(anyw, vmem),
        scratch_shapes=[
            pltpu.VMEM((256, cols), f32),
            pltpu.VMEM((4, 4, 8, 128), f32),
            pltpu.SemaphoreType.DMA,
        ],
        compiler_params=pltpu.CompilerParams(vmem_limit_bytes=56 << 20),
        name="decode",
    )(newmom, vals, iu, iv, dth, dtl, dch, dcl)


def per_device(hidden_act, out_grads, momentum, coeff_index):
    newmom, vals, iu, iv = exchange(out_grads, hidden_act, momentum, coeff_index)
    return decode(newmom, vals, iu, iv)


def solution(mesh):
    placed = (
        P("rep", None, "tp"),
        P("rep", "tp", None),
        P("rep", "tp", None),
        P(None, "tp", None, None),
    )
    return jax.shard_map(
        per_device,
        mesh=mesh,
        in_specs=placed,
        out_specs=(P("rep", "tp", None), P("tp", None)),
        check_vma=False,
    )
```

```python
import functools

import jax
import jax.numpy as jnp
import ml_dtypes
import numpy as np
from jax import lax
from jax.experimental import pallas as pl
from jax.experimental.pallas import tpu as pltpu
from jax.sharding import PartitionSpec as P

SPAN = 64
DECAY = 0.9
PIECES = 4
EARLY = 2
MESH = pl.DeviceIdType.MESH
f32, bf16, i32 = jnp.float32, jnp.bfloat16, jnp.int32


def dct_table():
    n = np.arange(SPAN)
    u = np.arange(SPAN)[:, None]
    scale = np.where(u == 0, np.sqrt(1.0 / SPAN), np.sqrt(2.0 / SPAN))
    return (scale * np.cos(np.pi * (2 * n[None] + 1) * u / (2 * SPAN))).astype(np.float32)


def split_table(x):
    high = x.astype(ml_dtypes.bfloat16)
    low = (x - high.astype(np.float32)).astype(ml_dtypes.bfloat16)
    return high, low


def split(x):
    high = x.astype(bf16)
    return high, (x - high.astype(f32)).astype(bf16)


def dot(a, b):
    return jnp.dot(a, b, preferred_element_type=f32)


def dot_t(a, b):
    return lax.dot_general(a, b, (((1,), (1,)), ((), ())), preferred_element_type=f32)


def dot3(ah, al, bh, bl):
    return dot(ah, bh) + dot(al, bh) + dot(ah, bl)


def lane_gather(x, idx):
    return jnp.take_along_axis(x, idx, axis=1, mode="promise_in_bounds")


def exchange_kernel(
    og_hbm, act_hbm, mom_hbm, idx_hbm, dth_hbm, dtl_hbm, dch_hbm, dcl_hbm, ct2_hbm,
    newmom_hbm, upd_hbm, vals, iuv,
    act, og, gt, mixed, idx, cu, rh, rl, wrow, dth, dtl, dch, dcl, ct2, upd, s_a, s_b, v_a, v_b,
    load_sem, og_send, og_recv, core_recv, v_send, v_recv, out_sem,
):
    rep, tp = lax.axis_index("rep"), lax.axis_index("tp")
    y, zl = rep // 4, rep % 4
    zh, x, c = tp // 8, (tp // 2) % 4, tp % 2
    tok = og_hbm.shape[1]

    def tpid(zh_, x_, c_):
        return (zh_ * 4 + x_) * 2 + c_

    xs = [lax.rem(x + 1, 4), lax.rem(x + 3, 4), lax.rem(x + 2, 4)]
    x_peers = [tpid(zh, xx, c) for xx in xs]
    core_peer = tpid(zh, x, 1 - c)
    z_peer = tpid(1 - zh, x, c)
    z_reps = [y * 4 + lax.rem(zl + d, 4) for d in (1, 2, 3)]
    y_reps = [lax.rem(y + d, 4) * 4 + zl for d in (1, 3, 2)]
    far_reps = [lax.rem(y + d, 4) * 4 + lax.rem(zl + e, 4) for d in (1, 3, 2) for e in (1, 2, 3)]
    all_reps = z_reps + y_reps + far_reps

    barrier = pltpu.get_barrier_semaphore()
    for t in x_peers + [core_peer, z_peer]:
        pl.semaphore_signal(barrier, inc=1, device_id=(rep, t), device_id_type=MESH)
    for r in all_reps:
        pl.semaphore_signal(barrier, inc=1, device_id=(r, tp), device_id_type=MESH)

    loads = []

    def load(src, dst):
        cp = pltpu.make_async_copy(src, dst, load_sem.at[len(loads)])
        cp.start()
        loads.append(cp)
        return cp

    def slot(t):
        return pl.ds(pl.multiple_of(t * tok, tok), tok)

    og_in = load(og_hbm.at[0], og.at[slot(tp)])
    idx_in = load(idx_hbm, idx)
    ct2_in = load(ct2_hbm, ct2)
    half = 4 * 2 * tok
    act_in = []
    for h in (zh, 1 - zh):
        rows = pl.ds(pl.multiple_of(h * half, half), half)
        act_in.append(load(act_hbm.at[0, rows], act.at[rows]))
    mom_in = load(mom_hbm.at[0], mixed)
    table_in = [load(dth_hbm, dth), load(dtl_hbm, dtl), load(dch_hbm, dch), load(dcl_hbm, dcl)]

    pl.semaphore_wait(barrier, 5 + len(all_reps))

    sends = []
    size = tok // PIECES

    def piece_copy(src_tp, dst_tp, p, k):
        rows = pl.ds(pl.multiple_of(src_tp * tok + p * size, size), size)
        return pltpu.make_async_remote_copy(
            src_ref=og.at[rows],
            dst_ref=og.at[rows],
            send_sem=og_send.at[k],
            recv_sem=og_recv.at[src_tp, p],
            device_id=(rep, dst_tp),
            device_id_type=MESH,
        )

    def core_copy(src_tp, k):
        return pltpu.make_async_remote_copy(
            src_ref=og.at[slot(src_tp)],
            dst_ref=og.at[slot(src_tp)],
            send_sem=og_send.at[k],
            recv_sem=core_recv.at[src_tp],
            device_id=(rep, core_peer),
            device_id_type=MESH,
        )

    def send(src_tp, dst_tp, p):
        cp = piece_copy(src_tp, dst_tp, p, len(sends))
        cp.start()
        sends.append(cp)

    def send_core(src_tp):
        cp = core_copy(src_tp, len(sends))
        cp.start()
        sends.append(cp)

    def arrived(src_tp, p):
        piece_copy(src_tp, tp, p, 0).wait_recv()

    def arrived_core(src_tp):
        core_copy(src_tp, 0).wait_recv()

    og_in.wait()
    for p in range(PIECES):
        send(tp, z_peer, p)
        for t in x_peers:
            send(tp, t, p)
    send_core(tp)

    idx_in.wait()
    ct2_in.wait()

    def index_rows(a, _):
        for b in range(6):
            got = idx[a, b]
            row = jnp.concatenate([got[4 * i : 4 * i + 4] for i in range(4)], axis=1)
            iuv[a, b] = jnp.concatenate([row >> 6, row & 63], axis=0).astype(f32)
        return 0

    lax.fori_loop(0, 28, index_rows, 0)

    def own_tables(j, _):
        row_b = lax.broadcasted_iota(i32, (128, 128), 0) // 64
        lane = lax.broadcasted_iota(i32, (128, 128), 1)
        mine = row_b == (lane // 32) % 2
        for q in range(6):
            a2, bp = q // 3, q % 3
            row = jnp.concatenate(
                [idx[4 * j + 2 * a2 + ap, 2 * bp + b, pl.ds(rep, 1), :] for ap in range(2) for b in range(2)],
                axis=1,
            )
            k = j * 6 + q
            cu[k] = lane_gather(ct2[...], jnp.broadcast_to(row >> 6, (64, 128)))
            cv = lane_gather(ct2[...], jnp.broadcast_to(row & 63, (64, 128)))
            cvh, cvl = split(jnp.where(mine, jnp.concatenate([cv, cv], axis=0), 0.0))
            rh[k] = cvh
            rl[k] = cvl
        return 0

    for p in range(PIECES):
        arrived(z_peer, p)
        for t in x_peers:
            send(z_peer, t, p)
        lax.fori_loop(7 * p // PIECES, 7 * (p + 1) // PIECES, own_tables, 0)
    send_core(z_peer)
    for t in x_peers:
        for p in range(PIECES):
            arrived(t, p)
        send_core(t)

    arrived_core(core_peer)
    for xx in xs:
        arrived_core(tpid(zh, xx, 1 - c))
    act_in[0].wait()

    def partial_grad(off, depth, first):
        off = pl.multiple_of(off, depth)
        bt = og[pl.ds(off, depth), :].T

        def body(j, _):
            cols = pl.ds(pl.multiple_of(j * 256, 256), 256)
            part = dot(bt, act[pl.ds(off, depth), cols])
            gt[:, cols] = part if first else gt[:, cols] + part
            return 0

        lax.fori_loop(0, 7, body, 0)

    partial_grad(zh * half, half, True)

    for xx in xs:
        t = tpid(1 - zh, xx, c)
        for p in range(PIECES):
            arrived(t, p)
        send_core(t)
    act_in[1].wait()
    mom_in.wait()
    for cp in table_in:
        cp.wait()
    arrived_core(tpid(1 - zh, x, 1 - c))
    for xx in xs:
        arrived_core(tpid(1 - zh, xx, 1 - c))

    off2 = pl.multiple_of((1 - zh) * half, half)
    bt2 = og[pl.ds(off2, half), :].T

    def forward(j):
        cols = slice(j * 256, j * 256 + 256)
        g = gt[:, cols] + dot(bt2, act[pl.ds(off2, half), cols])
        m = DECAY * mixed[cols, :] + g.T
        mixed[cols, :] = m
        mh, ml = split(m)
        lane = lax.broadcasted_iota(i32, (64, 128), 1)
        ws = []
        hs = [dot3(mh[:, :256], ml[:, :256], dth[...], dtl[...])]
        hs.append(dot3(mh[:, 256:], ml[:, 256:], dth[:128, :128], dtl[:128, :128]))
        hs = [hs[0][:, :128], hs[0][:, 128:], hs[1]]
        for q in range(6):
            a2, bp = q // 3, q % 3
            row = jnp.concatenate(
                [
                    (idx[4 * j + 2 * a2 + ap, 2 * bp + b, pl.ds(rep, 1), :] & 63) + 64 * b
                    for ap in range(2)
                    for b in range(2)
                ],
                axis=1,
            )
            ib = jnp.broadcast_to(row, (64, 128))
            h = hs[bp][128 * a2 : 128 * a2 + 128]
            got = jnp.where(lane < 64, lane_gather(h[:64], ib), lane_gather(h[64:], ib))
            w = jnp.sum(got * cu[j * 6 + q], axis=0, keepdims=True)
            wrow[j * 6 + q : j * 6 + q + 1, :] = w
            ws.append(w)
        rows = []
        for b in range(6):
            bp, bo = b // 2, 32 * (b % 2)
            rows.append(
                jnp.concatenate([ws[3 * a2 + bp][:, o + bo : o + bo + 32] for a2 in range(2) for o in (0, 64)], axis=1)
            )
        vals[rep, j] = jnp.concatenate(rows + [jnp.zeros((2, 128), f32)], axis=0)

    def vcopy(r, to, lo, n, si, ri):
        return pltpu.make_async_remote_copy(
            src_ref=vals.at[r, pl.ds(lo, n)],
            dst_ref=vals.at[r, pl.ds(lo, n)],
            send_sem=v_send.at[si],
            recv_sem=v_recv.at[r, ri],
            device_id=(to, tp),
            device_id_type=MESH,
        )

    groups = [(0, 4), (4, 2), (6, 1)]
    vsends = []

    def vsend(r, to, gi):
        cp = vcopy(r, to, *groups[gi], len(vsends), gi)
        cp.start()
        vsends.append(cp)

    def varrived(r, gi):
        vcopy(r, rep, *groups[gi], 0, gi).wait_recv()

    for j in range(4):
        forward(j)
    for r in z_reps + y_reps:
        vsend(rep, r, 0)
    for j in range(4, 6):
        forward(j)
    for r in z_reps + y_reps:
        vsend(rep, r, 1)
    for z in z_reps:
        varrived(z, 0)
        for r in y_reps:
            vsend(z, r, 0)
    forward(6)
    for r in all_reps:
        vsend(rep, r, 2)

    outs = []

    def keep(j):
        lane = lax.broadcasted_iota(i32, (64, 128), 1)
        for q in range(6):
            a2, bp = q // 3, q % 3
            k = j * 6 + q
            l = cu[k] * jnp.broadcast_to(wrow[k : k + 1, :], (64, 128))
            lh, ll = split(jnp.concatenate([jnp.where(lane < 64, l, 0.0), jnp.where(lane < 64, 0.0, l)], axis=0))
            kept = dot_t(lh, rh[k]) + dot_t(ll, rh[k]) + dot_t(lh, rl[k])
            rows = slice(j * 256 + a2 * 128, j * 256 + a2 * 128 + 128)
            cols = slice(bp * 128, bp * 128 + 128)
            mixed[rows, cols] = mixed[rows, cols] - kept

    def write(src, dst, lo, n):
        rows = pl.ds(lo * 256, n * 256)
        cp = pltpu.make_async_copy(src.at[rows], dst.at[rows], out_sem.at[len(outs)])
        cp.start()
        outs.append(cp)

    for j in range(4):
        keep(j)
    write(mixed, newmom_hbm, 0, 4)
    for z in z_reps:
        varrived(z, 1)
        for r in y_reps:
            vsend(z, r, 1)
    for j in range(4, 7):
        keep(j)
    write(mixed, newmom_hbm, 4, 3)

    for r in y_reps + far_reps:
        varrived(r, 0)
    if EARLY:
        decode_chunks(0, EARLY, vals, iuv, (dth, dtl, dch, dcl), upd, (s_a, s_b), (v_a, v_b))
        write(upd, upd_hbm, 0, EARLY)
    for r in y_reps + far_reps:
        varrived(r, 1)
    for r in all_reps:
        varrived(r, 2)
    for cp in sends + vsends:
        cp.wait_send()
    for cp in outs:
        cp.wait()


def exchange(og, act, mom, idx):
    rows, cols = mom.shape[1:]
    tok = act.shape[1]
    table = dct_table()
    dt = np.kron(np.eye(4, dtype=np.float32), table.T)
    tables = split_table(dt) + split_table(dt.T.copy())
    ct2 = np.concatenate([table.T, table.T], axis=1)
    vmem = pl.BlockSpec(memory_space=pltpu.VMEM)
    anyw = pl.BlockSpec(memory_space=pl.ANY)
    S = jax.ShapeDtypeStruct
    return pl.pallas_call(
        exchange_kernel,
        out_shape=(
            S((rows, cols), f32),
            S((max(EARLY, 1) * 256, cols), bf16),
            S((16, 7, 8, 128), f32),
            S((28, 6, 8, 128), f32),
        ),
        in_specs=[anyw] * 9,
        out_specs=(anyw, anyw, vmem, vmem),
        scratch_shapes=[
            pltpu.VMEM((tok, rows), bf16),
            pltpu.VMEM((tok, cols), bf16),
            pltpu.VMEM((cols, rows), f32),
            pltpu.VMEM((rows, cols), f32),
            pltpu.VMEM(idx.shape, i32),
            pltpu.VMEM((42, 64, 128), f32),
            pltpu.VMEM((42, 128, 128), bf16),
            pltpu.VMEM((42, 128, 128), bf16),
            pltpu.VMEM((48, 128), f32),
        ]
        + [pltpu.VMEM((256, 256), bf16)] * 4
        + [
            pltpu.VMEM((64, 128), f32),
            pltpu.VMEM((max(EARLY, 1) * 256, cols), bf16),
            pltpu.VMEM((256, cols), f32),
            pltpu.VMEM((256, cols), f32),
            pltpu.VMEM((4, 4, 8, 128), f32),
            pltpu.VMEM((4, 4, 8, 128), f32),
            pltpu.SemaphoreType.DMA((10,)),
            pltpu.SemaphoreType.DMA((8 + 7 * PIECES,)),
            pltpu.SemaphoreType.DMA((16, PIECES)),
            pltpu.SemaphoreType.DMA((16,)),
            pltpu.SemaphoreType.DMA((45,)),
            pltpu.SemaphoreType.DMA((16, 3)),
            pltpu.SemaphoreType.DMA((3,)),
        ],
        compiler_params=pltpu.CompilerParams(collective_id=0, has_side_effects=True, vmem_limit_bytes=56 << 20),
        name="exchange",
    )(og, act, mom, idx, *tables, ct2)


def decode_chunks(first, last, vals, iuv, tables, update, s_bufs, v_bufs):
    dth, dtl, dch, dcl = tables
    io = lax.broadcasted_iota(i32, (64, 128), 0).astype(f32).astype(bf16)
    io2 = lax.broadcasted_iota(i32, (128, 128), 0).astype(f32).astype(bf16)
    zero, zero2 = jnp.zeros((64, 128), bf16), jnp.zeros((128, 128), bf16)
    one2 = jnp.ones((128, 128), bf16)
    lane = lax.broadcasted_iota(i32, (1, 128), 1)

    def spread(row, n):
        return jnp.broadcast_to(row, (n, 128)).astype(bf16)

    def scatter(j):
        s_buf, v_buf = s_bufs[j % 2], v_bufs[j % 2]
        for g in range(4):
            got = [vals[4 * i + g, j] for i in range(4)]
            for ai in range(4):
                v_buf[ai, g] = jnp.concatenate([v[:, 32 * ai : 32 * ai + 32] for v in got], axis=1)
        for ai in range(4):
            for bp in range(3):
                left, right = [], []
                for bo in range(2):
                    b = 2 * bp + bo
                    for g in range(4):
                        hit = spread(iuv[4 * j + ai, b, g : g + 1, :], 64) == io
                        v = v_buf[ai, g, b : b + 1, :]
                        vh = v.astype(bf16).astype(f32)
                        left.append(
                            jnp.concatenate(
                                [jnp.where(hit, spread(vh, 64), zero), jnp.where(hit, spread(v - vh, 64), zero)], axis=0
                            )
                        )
                        at = spread(iuv[4 * j + ai, b, 4 + g : 5 + g, :] + 64.0 * bo, 128)
                        right.append(jnp.where(at == io2, one2, zero2))
                o = dot_t(jnp.concatenate(left, axis=1), jnp.concatenate(right, axis=1))
                s_buf[64 * ai : 64 * ai + 64, 128 * bp : 128 * bp + 128] = o[:64] + o[64:]

    def inverse(j):
        sh, sl = split(s_bufs[j % 2][...])
        t = jnp.concatenate(
            [
                dot3(sh[:, :256], sl[:, :256], dch[...], dcl[...]),
                dot3(sh[:, 256:], sl[:, 256:], dch[:128, :128], dcl[:128, :128]),
            ],
            axis=1,
        )
        th, tl = split(t)
        d = dot3(dth[...], dtl[...], th, tl)
        for ai in range(4):
            for bp in range(3):
                blk = d[64 * ai : 64 * ai + 64, 128 * bp : 128 * bp + 128]
                col = jnp.sum(blk * blk, axis=0, keepdims=True)
                lo = jnp.sum(jnp.where(lane < 64, col, 0.0), axis=1, keepdims=True)
                hi = jnp.sum(jnp.where(lane < 64, 0.0, col), axis=1, keepdims=True)
                q = jnp.where(lane < 64, lo, hi) * (1.0 / (SPAN * SPAN))
                r0 = j * 256 + 64 * ai
                update[r0 : r0 + 64, 128 * bp : 128 * bp + 128] = jnp.tanh(blk * lax.rsqrt(q + 1e-06)).astype(bf16)

    scatter(first)
    for j in range(first, last):
        if j + 1 < last:
            scatter(j + 1)
        inverse(j)


def decode_kernel(
    newmom_in, upd_in, vals, iuv, dth, dtl, dch, dcl, newmom, update, m_buf, upd, s_a, s_b, v_a, v_b, sem
):
    rows = m_buf.shape[0]
    early = pl.ds(0, EARLY * 256)
    late = pl.ds(EARLY * 256, rows - EARLY * 256)
    m_in = pltpu.make_async_copy(newmom_in, m_buf, sem.at[0])
    m_out = pltpu.make_async_copy(m_buf, newmom.at[0], sem.at[1])
    m_in.start()
    if EARLY:
        u_in = pltpu.make_async_copy(upd_in, upd.at[early], sem.at[2])
        u_out = pltpu.make_async_copy(upd.at[early], update.at[early], sem.at[3])
        u_in.start()
    mid = EARLY + 1
    decode_chunks(EARLY, mid, vals, iuv, (dth, dtl, dch, dcl), upd, (s_a, s_b), (v_a, v_b))
    m_in.wait()
    m_out.start()
    if EARLY:
        u_in.wait()
        u_out.start()
    decode_chunks(mid, 7, vals, iuv, (dth, dtl, dch, dcl), upd, (s_a, s_b), (v_a, v_b))
    last = pltpu.make_async_copy(upd.at[late], update.at[late], sem.at[4])
    last.start()
    m_out.wait()
    if EARLY:
        u_out.wait()
    last.wait()


def decode(newmom, upd, vals, iuv):
    rows, cols = newmom.shape
    table = dct_table()
    dt = np.kron(np.eye(4, dtype=np.float32), table.T)
    tables = split_table(dt) + split_table(dt.T.copy())
    vmem = pl.BlockSpec(memory_space=pltpu.VMEM)
    anyw = pl.BlockSpec(memory_space=pl.ANY)
    S = jax.ShapeDtypeStruct
    return pl.pallas_call(
        decode_kernel,
        out_shape=(S((1, rows, cols), f32), S((rows, cols), bf16)),
        in_specs=[anyw] * 2 + [vmem] * 6,
        out_specs=(anyw, anyw),
        scratch_shapes=[
            pltpu.VMEM((rows, cols), f32),
            pltpu.VMEM((rows, cols), bf16),
            pltpu.VMEM((256, cols), f32),
            pltpu.VMEM((256, cols), f32),
            pltpu.VMEM((4, 4, 8, 128), f32),
            pltpu.VMEM((4, 4, 8, 128), f32),
            pltpu.SemaphoreType.DMA((5,)),
        ],
        compiler_params=pltpu.CompilerParams(vmem_limit_bytes=56 << 20),
        name="decode",
    )(newmom, upd, vals, iuv, *tables)


def per_device(hidden_act, out_grads, momentum, coeff_index):
    newmom, upd, vals, iuv = exchange(out_grads, hidden_act, momentum, coeff_index.transpose(1, 2, 0, 3))
    return decode(newmom, upd, vals, iuv)


def solution(mesh):
    placed = (
        P("rep", None, "tp"),
        P("rep", "tp", None),
        P("rep", "tp", None),
        P(None, "tp", None, None),
    )
    return jax.shard_map(
        per_device,
        mesh=mesh,
        in_specs=placed,
        out_specs=(P("rep", "tp", None), P("tp", None)),
        check_vma=False,
    )
```

```python
import functools

import jax
import jax.numpy as jnp
import ml_dtypes
import numpy as np
from jax import lax
from jax.experimental import pallas as pl
from jax.experimental.pallas import tpu as pltpu
from jax.sharding import PartitionSpec as P

SPAN = 64
DECAY = 0.9
PIECES = 4
EARLY = 2
MESH = pl.DeviceIdType.MESH
f32, bf16, i32 = jnp.float32, jnp.bfloat16, jnp.int32


def dct_table():
    n = np.arange(SPAN)
    u = np.arange(SPAN)[:, None]
    scale = np.where(u == 0, np.sqrt(1.0 / SPAN), np.sqrt(2.0 / SPAN))
    return (scale * np.cos(np.pi * (2 * n[None] + 1) * u / (2 * SPAN))).astype(np.float32)


def split_table(x):
    high = x.astype(ml_dtypes.bfloat16)
    low = (x - high.astype(np.float32)).astype(ml_dtypes.bfloat16)
    return high, low


def split(x):
    high = x.astype(bf16)
    return high, (x - high.astype(f32)).astype(bf16)


def dot(a, b):
    return jnp.dot(a, b, preferred_element_type=f32)


def dot_t(a, b):
    return lax.dot_general(a, b, (((1,), (1,)), ((), ())), preferred_element_type=f32)


def dot3(ah, al, bh, bl):
    return dot(ah, bh) + dot(al, bh) + dot(ah, bl)


def lane_gather(x, idx):
    return jnp.take_along_axis(x, idx, axis=1, mode="promise_in_bounds")


def exchange_kernel(
    og_hbm, act_hbm, mom_hbm, idx_hbm, dth_hbm, dtl_hbm, dch_hbm, dcl_hbm, ct2_hbm,
    mixed, upd, vals, iuv,
    act, og, gt, idx, cu, rh, rl, wrow, dth, dtl, dch, dcl, ct2, s_a, s_b, v_a, v_b,
    load_sem, og_send, og_recv, core_recv, v_send, v_recv,
):
    rep, tp = lax.axis_index("rep"), lax.axis_index("tp")
    y, zl = rep // 4, rep % 4
    zh, x, c = tp // 8, (tp // 2) % 4, tp % 2
    tok = og_hbm.shape[1]

    def tpid(zh_, x_, c_):
        return (zh_ * 4 + x_) * 2 + c_

    xs = [lax.rem(x + 1, 4), lax.rem(x + 3, 4), lax.rem(x + 2, 4)]
    x_peers = [tpid(zh, xx, c) for xx in xs]
    core_peer = tpid(zh, x, 1 - c)
    z_peer = tpid(1 - zh, x, c)
    z_reps = [y * 4 + lax.rem(zl + d, 4) for d in (1, 2, 3)]
    y_reps = [lax.rem(y + d, 4) * 4 + zl for d in (1, 3, 2)]
    far_reps = [lax.rem(y + d, 4) * 4 + lax.rem(zl + e, 4) for d in (1, 3, 2) for e in (1, 2, 3)]
    all_reps = z_reps + y_reps + far_reps

    barrier = pltpu.get_barrier_semaphore()
    for t in x_peers + [core_peer, z_peer]:
        pl.semaphore_signal(barrier, inc=1, device_id=(rep, t), device_id_type=MESH)
    for r in all_reps:
        pl.semaphore_signal(barrier, inc=1, device_id=(r, tp), device_id_type=MESH)

    loads = []

    def load(src, dst):
        cp = pltpu.make_async_copy(src, dst, load_sem.at[len(loads)])
        cp.start()
        loads.append(cp)
        return cp

    def slot(t):
        return pl.ds(pl.multiple_of(t * tok, tok), tok)

    og_in = load(og_hbm.at[0], og.at[slot(tp)])
    idx_in = load(idx_hbm, idx)
    ct2_in = load(ct2_hbm, ct2)
    half = 4 * 2 * tok
    act_in = []
    for h in (zh, 1 - zh):
        rows = pl.ds(pl.multiple_of(h * half, half), half)
        act_in.append(load(act_hbm.at[0, rows], act.at[rows]))
    mom_in = load(mom_hbm.at[0], mixed)
    table_in = [load(dth_hbm, dth), load(dtl_hbm, dtl), load(dch_hbm, dch), load(dcl_hbm, dcl)]

    pl.semaphore_wait(barrier, 5 + len(all_reps))

    sends = []
    size = tok // PIECES

    def piece_copy(src_tp, dst_tp, p, k):
        rows = pl.ds(pl.multiple_of(src_tp * tok + p * size, size), size)
        return pltpu.make_async_remote_copy(
            src_ref=og.at[rows],
            dst_ref=og.at[rows],
            send_sem=og_send.at[k],
            recv_sem=og_recv.at[src_tp, p],
            device_id=(rep, dst_tp),
            device_id_type=MESH,
        )

    def core_copy(src_tp, k):
        return pltpu.make_async_remote_copy(
            src_ref=og.at[slot(src_tp)],
            dst_ref=og.at[slot(src_tp)],
            send_sem=og_send.at[k],
            recv_sem=core_recv.at[src_tp],
            device_id=(rep, core_peer),
            device_id_type=MESH,
        )

    def send(src_tp, dst_tp, p):
        cp = piece_copy(src_tp, dst_tp, p, len(sends))
        cp.start()
        sends.append(cp)

    def send_core(src_tp):
        cp = core_copy(src_tp, len(sends))
        cp.start()
        sends.append(cp)

    def arrived(src_tp, p):
        piece_copy(src_tp, tp, p, 0).wait_recv()

    def arrived_core(src_tp):
        core_copy(src_tp, 0).wait_recv()

    og_in.wait()
    for p in range(PIECES):
        send(tp, z_peer, p)
        for t in x_peers:
            send(tp, t, p)
    send_core(tp)

    idx_in.wait()
    ct2_in.wait()

    def index_rows(a, _):
        for b in range(6):
            got = idx[a, b]
            row = jnp.concatenate([got[4 * i : 4 * i + 4] for i in range(4)], axis=1)
            iuv[a, b] = jnp.concatenate([row >> 6, row & 63], axis=0).astype(f32)
        return 0

    lax.fori_loop(0, 28, index_rows, 0)

    def own_tables(j, _):
        row_b = lax.broadcasted_iota(i32, (128, 128), 0) // 64
        lane = lax.broadcasted_iota(i32, (128, 128), 1)
        mine = row_b == (lane // 32) % 2
        for q in range(6):
            a2, bp = q // 3, q % 3
            row = jnp.concatenate(
                [idx[4 * j + 2 * a2 + ap, 2 * bp + b, pl.ds(rep, 1), :] for ap in range(2) for b in range(2)],
                axis=1,
            )
            k = j * 6 + q
            cu[k] = lane_gather(ct2[...], jnp.broadcast_to(row >> 6, (64, 128)))
            cv = lane_gather(ct2[...], jnp.broadcast_to(row & 63, (64, 128)))
            cvh, cvl = split(jnp.where(mine, jnp.concatenate([cv, cv], axis=0), 0.0))
            rh[k] = cvh
            rl[k] = cvl
        return 0

    for p in range(PIECES):
        arrived(z_peer, p)
        for t in x_peers:
            send(z_peer, t, p)
        lax.fori_loop(7 * p // PIECES, 7 * (p + 1) // PIECES, own_tables, 0)
    send_core(z_peer)
    for t in x_peers:
        for p in range(PIECES):
            arrived(t, p)
        send_core(t)

    arrived_core(core_peer)
    for xx in xs:
        arrived_core(tpid(zh, xx, 1 - c))
    act_in[0].wait()

    def partial_grad(off, depth, first):
        off = pl.multiple_of(off, depth)
        bt = og[pl.ds(off, depth), :].T

        def body(j, _):
            cols = pl.ds(pl.multiple_of(j * 256, 256), 256)
            part = dot(bt, act[pl.ds(off, depth), cols])
            gt[:, cols] = part if first else gt[:, cols] + part
            return 0

        lax.fori_loop(0, 7, body, 0)

    partial_grad(zh * half, half, True)

    for xx in xs:
        t = tpid(1 - zh, xx, c)
        for p in range(PIECES):
            arrived(t, p)
        send_core(t)
    act_in[1].wait()

    mom_in.wait()
    for cp in table_in:
        cp.wait()
    arrived_core(tpid(1 - zh, x, 1 - c))
    for xx in xs:
        arrived_core(tpid(1 - zh, xx, 1 - c))

    off2 = pl.multiple_of((1 - zh) * half, half)
    bt2 = og[pl.ds(off2, half), :].T

    def forward(j):
        cols = slice(j * 256, j * 256 + 256)
        g = gt[:, cols] + dot(bt2, act[pl.ds(off2, half), cols])
        m = DECAY * mixed[cols, :] + g.T
        mixed[cols, :] = m
        mh, ml = split(m)
        lane = lax.broadcasted_iota(i32, (64, 128), 1)
        ws = []
        hs = [dot3(mh[:, :256], ml[:, :256], dth[...], dtl[...])]
        hs.append(dot3(mh[:, 256:], ml[:, 256:], dth[:128, :128], dtl[:128, :128]))
        hs = [hs[0][:, :128], hs[0][:, 128:], hs[1]]
        for q in range(6):
            a2, bp = q // 3, q % 3
            row = jnp.concatenate(
                [
                    (idx[4 * j + 2 * a2 + ap, 2 * bp + b, pl.ds(rep, 1), :] & 63) + 64 * b
                    for ap in range(2)
                    for b in range(2)
                ],
                axis=1,
            )
            ib = jnp.broadcast_to(row, (64, 128))
            h = hs[bp][128 * a2 : 128 * a2 + 128]
            got = jnp.where(lane < 64, lane_gather(h[:64], ib), lane_gather(h[64:], ib))
            w = jnp.sum(got * cu[j * 6 + q], axis=0, keepdims=True)
            wrow[j * 6 + q : j * 6 + q + 1, :] = w
            ws.append(w)
        rows = []
        for b in range(6):
            bp, bo = b // 2, 32 * (b % 2)
            rows.append(
                jnp.concatenate([ws[3 * a2 + bp][:, o + bo : o + bo + 32] for a2 in range(2) for o in (0, 64)], axis=1)
            )
        vals[rep, j] = jnp.concatenate(rows + [jnp.zeros((2, 128), f32)], axis=0)

    def vcopy(r, to, lo, n, si, ri):
        return pltpu.make_async_remote_copy(
            src_ref=vals.at[r, pl.ds(lo, n)],
            dst_ref=vals.at[r, pl.ds(lo, n)],
            send_sem=v_send.at[si],
            recv_sem=v_recv.at[r, ri],
            device_id=(to, tp),
            device_id_type=MESH,
        )

    groups = [(0, 4), (4, 2), (6, 1)]
    vsends = []

    def vsend(r, to, gi):
        cp = vcopy(r, to, *groups[gi], len(vsends), gi)
        cp.start()
        vsends.append(cp)

    def varrived(r, gi):
        vcopy(r, rep, *groups[gi], 0, gi).wait_recv()

    for j in range(4):
        forward(j)
    for r in z_reps + y_reps:
        vsend(rep, r, 0)
    for j in range(4, 6):
        forward(j)
    for r in z_reps + y_reps:
        vsend(rep, r, 1)
    for z in z_reps:
        varrived(z, 0)
        for r in y_reps:
            vsend(z, r, 0)
    forward(6)
    for r in all_reps:
        vsend(rep, r, 2)

    def keep(j):
        lane = lax.broadcasted_iota(i32, (64, 128), 1)
        for q in range(6):
            a2, bp = q // 3, q % 3
            k = j * 6 + q
            l = cu[k] * jnp.broadcast_to(wrow[k : k + 1, :], (64, 128))
            lh, ll = split(jnp.concatenate([jnp.where(lane < 64, l, 0.0), jnp.where(lane < 64, 0.0, l)], axis=0))
            kept = dot_t(lh, rh[k]) + dot_t(ll, rh[k]) + dot_t(lh, rl[k])
            rows = slice(j * 256 + a2 * 128, j * 256 + a2 * 128 + 128)
            cols = slice(bp * 128, bp * 128 + 128)
            mixed[rows, cols] = mixed[rows, cols] - kept

    for j in range(4):
        keep(j)
    for z in z_reps:
        varrived(z, 1)
        for r in y_reps:
            vsend(z, r, 1)
    for j in range(4, 7):
        keep(j)

    for r in y_reps + far_reps:
        varrived(r, 0)
    if EARLY:
        decode_chunks(0, EARLY, vals, iuv, (dth, dtl, dch, dcl), upd, (s_a, s_b), (v_a, v_b))
    for r in y_reps + far_reps:
        varrived(r, 1)
    for r in all_reps:
        varrived(r, 2)
    for cp in sends + vsends:
        cp.wait_send()


def exchange(og, act, mom, idx):
    rows, cols = mom.shape[1:]
    tok = act.shape[1]
    table = dct_table()
    dt = np.kron(np.eye(4, dtype=np.float32), table.T)
    tables = split_table(dt) + split_table(dt.T.copy())
    ct2 = np.concatenate([table.T, table.T], axis=1)
    vmem = pl.BlockSpec(memory_space=pltpu.VMEM)
    anyw = pl.BlockSpec(memory_space=pl.ANY)
    S = jax.ShapeDtypeStruct
    return pl.pallas_call(
        exchange_kernel,
        out_shape=(
            pltpu.VMEM((rows, cols), f32),
            pltpu.VMEM((EARLY * 256, cols), bf16),
            pltpu.VMEM((16, 7, 8, 128), f32),
            pltpu.VMEM((28, 6, 8, 128), f32),
        ),
        in_specs=[anyw] * 9,
        out_specs=(vmem, vmem, vmem, vmem),
        scratch_shapes=[
            pltpu.VMEM((tok, rows), bf16),
            pltpu.VMEM((tok, cols), bf16),
            pltpu.VMEM((cols, rows), f32),
            pltpu.VMEM(idx.shape, i32),
            pltpu.VMEM((42, 64, 128), f32),
            pltpu.VMEM((42, 128, 128), bf16),
            pltpu.VMEM((42, 128, 128), bf16),
            pltpu.VMEM((48, 128), f32),
        ]
        + [pltpu.VMEM((256, 256), bf16)] * 4
        + [
            pltpu.VMEM((64, 128), f32),
            pltpu.VMEM((256, cols), f32),
            pltpu.VMEM((256, cols), f32),
            pltpu.VMEM((4, 4, 8, 128), f32),
            pltpu.VMEM((4, 4, 8, 128), f32),
            pltpu.SemaphoreType.DMA((10,)),
            pltpu.SemaphoreType.DMA((8 + 7 * PIECES,)),
            pltpu.SemaphoreType.DMA((16, PIECES)),
            pltpu.SemaphoreType.DMA((16,)),
            pltpu.SemaphoreType.DMA((45,)),
            pltpu.SemaphoreType.DMA((16, 3)),
        ],
        compiler_params=pltpu.CompilerParams(collective_id=0, has_side_effects=True, vmem_limit_bytes=57 << 20),
        name="exchange",
    )(og, act, mom, idx, *tables, ct2)


def decode_chunks(first, last, vals, iuv, tables, update, s_bufs, v_bufs, ready=None, done=None):
    dth, dtl, dch, dcl = tables
    io = lax.broadcasted_iota(i32, (64, 128), 0).astype(f32).astype(bf16)
    io2 = lax.broadcasted_iota(i32, (128, 128), 0).astype(f32).astype(bf16)
    zero, zero2 = jnp.zeros((64, 128), bf16), jnp.zeros((128, 128), bf16)
    one2 = jnp.ones((128, 128), bf16)
    lane = lax.broadcasted_iota(i32, (1, 128), 1)

    def spread(row, n):
        return jnp.broadcast_to(row, (n, 128)).astype(bf16)

    def scatter(j):
        s_buf, v_buf = s_bufs[j % 2], v_bufs[j % 2]
        for g in range(4):
            got = [vals[4 * i + g, j] for i in range(4)]
            for ai in range(4):
                v_buf[ai, g] = jnp.concatenate([v[:, 32 * ai : 32 * ai + 32] for v in got], axis=1)
        for ai in range(4):
            for bp in range(3):
                left, right = [], []
                for bo in range(2):
                    b = 2 * bp + bo
                    for g in range(4):
                        hit = spread(iuv[4 * j + ai, b, g : g + 1, :], 64) == io
                        v = v_buf[ai, g, b : b + 1, :]
                        vh = v.astype(bf16).astype(f32)
                        left.append(
                            jnp.concatenate(
                                [jnp.where(hit, spread(vh, 64), zero), jnp.where(hit, spread(v - vh, 64), zero)], axis=0
                            )
                        )
                        at = spread(iuv[4 * j + ai, b, 4 + g : 5 + g, :] + 64.0 * bo, 128)
                        right.append(jnp.where(at == io2, one2, zero2))
                o = dot_t(jnp.concatenate(left, axis=1), jnp.concatenate(right, axis=1))
                s_buf[64 * ai : 64 * ai + 64, 128 * bp : 128 * bp + 128] = o[:64] + o[64:]

    def inverse(j):
        sh, sl = split(s_bufs[j % 2][...])
        t = jnp.concatenate(
            [
                dot3(sh[:, :256], sl[:, :256], dch[...], dcl[...]),
                dot3(sh[:, 256:], sl[:, 256:], dch[:128, :128], dcl[:128, :128]),
            ],
            axis=1,
        )
        th, tl = split(t)
        d = dot3(dth[...], dtl[...], th, tl)
        for ai in range(4):
            for bp in range(3):
                blk = d[64 * ai : 64 * ai + 64, 128 * bp : 128 * bp + 128]
                col = jnp.sum(blk * blk, axis=0, keepdims=True)
                lo = jnp.sum(jnp.where(lane < 64, col, 0.0), axis=1, keepdims=True)
                hi = jnp.sum(jnp.where(lane < 64, 0.0, col), axis=1, keepdims=True)
                q = jnp.where(lane < 64, lo, hi) * (1.0 / (SPAN * SPAN))
                r0 = j * 256 + 64 * ai
                update[r0 : r0 + 64, 128 * bp : 128 * bp + 128] = jnp.tanh(blk * lax.rsqrt(q + 1e-06)).astype(bf16)

    scatter(first)
    if ready is not None:
        ready()
    for j in range(first, last):
        if j + 1 < last:
            scatter(j + 1)
        inverse(j)
        if done is not None:
            done(j)


def decode_kernel(
    newmom_in, upd_in, vals, iuv, dth_hbm, dtl_hbm, dch_hbm, dcl_hbm, newmom, update,
    upd, dth, dtl, dch, dcl, s_a, s_b, v_a, v_b, sem,
):
    tables = (dth, dtl, dch, dcl)
    loads = [
        pltpu.make_async_copy(src, dst, sem.at[9 + i])
        for i, (src, dst) in enumerate(zip((dth_hbm, dtl_hbm, dch_hbm, dcl_hbm), tables))
    ]
    early = pl.ds(0, EARLY * 256)
    outs = [
        pltpu.make_async_copy(newmom_in, newmom.at[0], sem.at[7]),
        pltpu.make_async_copy(upd_in, update.at[early], sem.at[8]),
    ]
    for cp in loads + outs:
        cp.start()

    def ready():
        for cp in loads:
            cp.wait()

    def done(j):
        rows = pl.ds(j * 256, 256)
        cp = pltpu.make_async_copy(upd.at[rows], update.at[rows], sem.at[j])
        cp.start()
        outs.append(cp)

    decode_chunks(EARLY, 7, vals, iuv, tables, upd, (s_a, s_b), (v_a, v_b), ready, done)
    for cp in outs:
        cp.wait()


def decode(newmom, upd, vals, iuv):
    rows, cols = newmom.shape
    table = dct_table()
    dt = np.kron(np.eye(4, dtype=np.float32), table.T)
    tables = split_table(dt) + split_table(dt.T.copy())
    vmem = pl.BlockSpec(memory_space=pltpu.VMEM)
    anyw = pl.BlockSpec(memory_space=pl.ANY)
    S = jax.ShapeDtypeStruct
    return pl.pallas_call(
        decode_kernel,
        out_shape=(S((1, rows, cols), f32), S((rows, cols), bf16)),
        in_specs=[vmem] * 4 + [anyw] * 4,
        out_specs=(anyw, anyw),
        scratch_shapes=[pltpu.VMEM((rows, cols), bf16)]
        + [pltpu.VMEM((256, 256), bf16)] * 4
        + [
            pltpu.VMEM((256, cols), f32),
            pltpu.VMEM((256, cols), f32),
            pltpu.VMEM((4, 4, 8, 128), f32),
            pltpu.VMEM((4, 4, 8, 128), f32),
            pltpu.SemaphoreType.DMA((13,)),
        ],
        compiler_params=pltpu.CompilerParams(vmem_limit_bytes=57 << 20),
        name="decode",
    )(newmom, upd, vals, iuv, *tables)


def per_device(hidden_act, out_grads, momentum, coeff_index):
    newmom, upd, vals, iuv = exchange(out_grads, hidden_act, momentum, coeff_index.transpose(1, 2, 0, 3))
    held = [pltpu.with_memory_space_constraint(v, pltpu.VMEM) for v in (newmom, upd, vals, iuv)]
    return decode(*held)


def solution(mesh):
    placed = (
        P("rep", None, "tp"),
        P("rep", "tp", None),
        P("rep", "tp", None),
        P(None, "tp", None, None),
    )
    return jax.shard_map(
        per_device,
        mesh=mesh,
        in_specs=placed,
        out_specs=(P("rep", "tp", None), P("tp", None)),
        check_vma=False,
    )
```

```python
import functools

import jax
import jax.numpy as jnp
import ml_dtypes
import numpy as np
from jax import lax
from jax.experimental import pallas as pl
from jax.experimental.pallas import tpu as pltpu
from jax.sharding import PartitionSpec as P

SPAN = 64
DECAY = 0.9
PIECES = 4
EARLY = 2
MESH = pl.DeviceIdType.MESH
f32, bf16, i32 = jnp.float32, jnp.bfloat16, jnp.int32


def dct_table():
    n = np.arange(SPAN)
    u = np.arange(SPAN)[:, None]
    scale = np.where(u == 0, np.sqrt(1.0 / SPAN), np.sqrt(2.0 / SPAN))
    return (scale * np.cos(np.pi * (2 * n[None] + 1) * u / (2 * SPAN))).astype(np.float32)


def split_table(x):
    high = x.astype(ml_dtypes.bfloat16)
    low = (x - high.astype(np.float32)).astype(ml_dtypes.bfloat16)
    return high, low


def split(x):
    high = x.astype(bf16)
    return high, (x - high.astype(f32)).astype(bf16)


def dot(a, b):
    return jnp.dot(a, b, preferred_element_type=f32)


def dot_t(a, b):
    return lax.dot_general(a, b, (((1,), (1,)), ((), ())), preferred_element_type=f32)


def dot3(ah, al, bh, bl):
    return dot(ah, bh) + dot(al, bh) + dot(ah, bl)


def lane_gather(x, idx):
    return jnp.take_along_axis(x, idx, axis=1, mode="promise_in_bounds")


def exchange_kernel(
    og_hbm, act_hbm, mom_hbm, idx_hbm, dth_hbm, dtl_hbm, dch_hbm, dcl_hbm, ct2_hbm,
    mixed, upd, vals, iuv,
    act, og, gt, idx, cu, rh, rl, wrow, dth, dtl, dch, dcl, ct2, s_a, s_b, v_a, v_b,
    load_sem, og_send, og_recv, core_recv, v_send, v_recv,
):
    rep, tp = lax.axis_index("rep"), lax.axis_index("tp")
    y, zl = rep // 4, rep % 4
    zh, x, c = tp // 8, (tp // 2) % 4, tp % 2
    tok = og_hbm.shape[1]

    def tpid(zh_, x_, c_):
        return (zh_ * 4 + x_) * 2 + c_

    xs = [lax.rem(x + 1, 4), lax.rem(x + 3, 4), lax.rem(x + 2, 4)]
    x_peers = [tpid(zh, xx, c) for xx in xs]
    core_peer = tpid(zh, x, 1 - c)
    z_peer = tpid(1 - zh, x, c)
    z_reps = [y * 4 + lax.rem(zl + d, 4) for d in (1, 2, 3)]
    y_reps = [lax.rem(y + d, 4) * 4 + zl for d in (1, 3, 2)]
    far_reps = [lax.rem(y + d, 4) * 4 + lax.rem(zl + e, 4) for d in (1, 3, 2) for e in (1, 2, 3)]
    all_reps = z_reps + y_reps + far_reps

    barrier = pltpu.get_barrier_semaphore()
    for t in x_peers + [core_peer, z_peer]:
        pl.semaphore_signal(barrier, inc=1, device_id=(rep, t), device_id_type=MESH)
    for r in all_reps:
        pl.semaphore_signal(barrier, inc=1, device_id=(r, tp), device_id_type=MESH)

    loads = []

    def load(src, dst):
        cp = pltpu.make_async_copy(src, dst, load_sem.at[len(loads)])
        cp.start()
        loads.append(cp)
        return cp

    def slot(t):
        return pl.ds(pl.multiple_of(t * tok, tok), tok)

    og_in = load(og_hbm.at[0], og.at[slot(tp)])
    idx_in = load(idx_hbm, idx)
    ct2_in = load(ct2_hbm, ct2)
    half = 4 * 2 * tok
    act_in = []
    for h in (zh, 1 - zh):
        rows = pl.ds(pl.multiple_of(h * half, half), half)
        act_in.append(load(act_hbm.at[0, rows], act.at[rows]))
    mom_in = load(mom_hbm.at[0], mixed)
    table_in = [load(dth_hbm, dth), load(dtl_hbm, dtl), load(dch_hbm, dch), load(dcl_hbm, dcl)]

    pl.semaphore_wait(barrier, 5 + len(all_reps))

    sends = []
    size = tok // PIECES

    def piece_copy(src_tp, dst_tp, p, k):
        rows = slot(src_tp) if p is None else pl.ds(pl.multiple_of(src_tp * tok + p * size, size), size)
        return pltpu.make_async_remote_copy(
            src_ref=og.at[rows],
            dst_ref=og.at[rows],
            send_sem=og_send.at[k],
            recv_sem=og_recv.at[src_tp, 0 if p is None else p],
            device_id=(rep, dst_tp),
            device_id_type=MESH,
        )

    def core_copy(src_tp, k):
        return pltpu.make_async_remote_copy(
            src_ref=og.at[slot(src_tp)],
            dst_ref=og.at[slot(src_tp)],
            send_sem=og_send.at[k],
            recv_sem=core_recv.at[src_tp],
            device_id=(rep, core_peer),
            device_id_type=MESH,
        )

    def send(src_tp, dst_tp, p):
        cp = piece_copy(src_tp, dst_tp, p, len(sends))
        cp.start()
        sends.append(cp)

    def send_core(src_tp):
        cp = core_copy(src_tp, len(sends))
        cp.start()
        sends.append(cp)

    def arrived(src_tp, p):
        piece_copy(src_tp, tp, p, 0).wait_recv()

    def arrived_core(src_tp):
        core_copy(src_tp, 0).wait_recv()

    og_in.wait()
    for p in range(PIECES):
        send(tp, z_peer, p)
    for t in x_peers:
        send(tp, t, None)
    send_core(tp)

    idx_in.wait()
    ct2_in.wait()

    def index_rows(a, _):
        for b in range(6):
            got = idx[a, b]
            row = jnp.concatenate([got[4 * i : 4 * i + 4] for i in range(4)], axis=1)
            iuv[a, b] = jnp.concatenate([row >> 6, row & 63], axis=0).astype(f32)
        return 0

    lax.fori_loop(0, 28, index_rows, 0)

    def own_tables(j, _):
        row_b = lax.broadcasted_iota(i32, (128, 128), 0) // 64
        lane = lax.broadcasted_iota(i32, (128, 128), 1)
        mine = row_b == (lane // 32) % 2
        for q in range(6):
            a2, bp = q // 3, q % 3
            row = jnp.concatenate(
                [idx[4 * j + 2 * a2 + ap, 2 * bp + b, pl.ds(rep, 1), :] for ap in range(2) for b in range(2)],
                axis=1,
            )
            k = j * 6 + q
            cu[k] = lane_gather(ct2[...], jnp.broadcast_to(row >> 6, (64, 128)))
            cv = lane_gather(ct2[...], jnp.broadcast_to(row & 63, (64, 128)))
            cvh, cvl = split(jnp.where(mine, jnp.concatenate([cv, cv], axis=0), 0.0))
            rh[k] = cvh
            rl[k] = cvl
        return 0

    lax.fori_loop(0, 7, own_tables, 0)
    for t in x_peers:
        arrived(t, None)
        send_core(t)
    for p in range(PIECES):
        arrived(z_peer, p)
        for t in x_peers:
            send(z_peer, t, p)
    send_core(z_peer)

    arrived_core(core_peer)
    for xx in xs:
        arrived_core(tpid(zh, xx, 1 - c))
    act_in[0].wait()

    def partial_grad(off, depth, first):
        off = pl.multiple_of(off, depth)
        bt = og[pl.ds(off, depth), :].T

        def body(j, _):
            cols = pl.ds(pl.multiple_of(j * 256, 256), 256)
            part = dot(bt, act[pl.ds(off, depth), cols])
            gt[:, cols] = part if first else gt[:, cols] + part
            return 0

        lax.fori_loop(0, 7, body, 0)

    partial_grad(zh * half, half, True)

    for xx in xs:
        t = tpid(1 - zh, xx, c)
        for p in range(PIECES):
            arrived(t, p)
        send_core(t)
    act_in[1].wait()

    def late_slots(core):
        return [slot(tpid(1 - zh, xx, core)) for xx in range(4)]

    mine = late_slots(c)
    bt1 = jnp.concatenate([og[r, :] for r in mine], axis=0).T

    def late_grad(j, _):
        cols = pl.ds(pl.multiple_of(j * 256, 256), 256)
        gt[:, cols] = gt[:, cols] + dot(bt1, jnp.concatenate([act[r, cols] for r in mine], axis=0))
        return 0

    lax.fori_loop(0, 7, late_grad, 0)

    mom_in.wait()
    for cp in table_in:
        cp.wait()
    arrived_core(tpid(1 - zh, x, 1 - c))
    for xx in xs:
        arrived_core(tpid(1 - zh, xx, 1 - c))

    theirs = late_slots(1 - c)
    bt2 = jnp.concatenate([og[r, :] for r in theirs], axis=0).T

    def forward(j):
        cols = slice(j * 256, j * 256 + 256)
        g = gt[:, cols] + dot(bt2, jnp.concatenate([act[r, cols] for r in theirs], axis=0))
        m = DECAY * mixed[cols, :] + g.T
        mixed[cols, :] = m
        mh, ml = split(m)
        lane = lax.broadcasted_iota(i32, (64, 128), 1)
        ws = []
        for q in range(6):
            a2, bp = q // 3, q % 3
            k = j * 6 + q
            rows = slice(128 * a2, 128 * a2 + 128)
            at = slice(128 * bp, 128 * bp + 128)
            t = dot(mh[rows, at], rh[k]) + dot(ml[rows, at], rh[k]) + dot(mh[rows, at], rl[k])
            got = jnp.where(lane < 64, t[:64], t[64:])
            w = jnp.sum(got * cu[j * 6 + q], axis=0, keepdims=True)
            wrow[j * 6 + q : j * 6 + q + 1, :] = w
            ws.append(w)
        rows = []
        for b in range(6):
            bp, bo = b // 2, 32 * (b % 2)
            rows.append(
                jnp.concatenate([ws[3 * a2 + bp][:, o + bo : o + bo + 32] for a2 in range(2) for o in (0, 64)], axis=1)
            )
        vals[rep, j] = jnp.concatenate(rows + [jnp.zeros((2, 128), f32)], axis=0)

    def vcopy(r, to, lo, n, si, ri):
        return pltpu.make_async_remote_copy(
            src_ref=vals.at[r, pl.ds(lo, n)],
            dst_ref=vals.at[r, pl.ds(lo, n)],
            send_sem=v_send.at[si],
            recv_sem=v_recv.at[r, ri],
            device_id=(to, tp),
            device_id_type=MESH,
        )

    groups = [(0, 4), (4, 2), (6, 1)]
    vsends = []

    def vsend(r, to, gi):
        cp = vcopy(r, to, *groups[gi], len(vsends), gi)
        cp.start()
        vsends.append(cp)

    def varrived(r, gi):
        vcopy(r, rep, *groups[gi], 0, gi).wait_recv()

    for j in range(4):
        forward(j)
    for r in z_reps + y_reps:
        vsend(rep, r, 0)
    for j in range(4, 6):
        forward(j)
    for r in z_reps + y_reps:
        vsend(rep, r, 1)
    for z in z_reps:
        varrived(z, 0)
        for r in y_reps:
            vsend(z, r, 0)
    forward(6)
    for r in all_reps:
        vsend(rep, r, 2)

    def keep(j):
        lane = lax.broadcasted_iota(i32, (64, 128), 1)
        for q in range(6):
            a2, bp = q // 3, q % 3
            k = j * 6 + q
            l = cu[k] * jnp.broadcast_to(wrow[k : k + 1, :], (64, 128))
            lh, ll = split(jnp.concatenate([jnp.where(lane < 64, l, 0.0), jnp.where(lane < 64, 0.0, l)], axis=0))
            kept = dot_t(lh, rh[k]) + dot_t(ll, rh[k]) + dot_t(lh, rl[k])
            rows = slice(j * 256 + a2 * 128, j * 256 + a2 * 128 + 128)
            cols = slice(bp * 128, bp * 128 + 128)
            mixed[rows, cols] = mixed[rows, cols] - kept

    for j in range(4):
        keep(j)
    for z in z_reps:
        varrived(z, 1)
        for r in y_reps:
            vsend(z, r, 1)
    for j in range(4, 7):
        keep(j)

    for r in y_reps + far_reps:
        varrived(r, 0)
    if EARLY:
        decode_chunks(0, EARLY, vals, iuv, (dth, dtl, dch, dcl), upd, (s_a, s_b), (v_a, v_b))
    for r in y_reps + far_reps:
        varrived(r, 1)
    for r in all_reps:
        varrived(r, 2)
    for cp in sends + vsends:
        cp.wait_send()


def exchange(og, act, mom, idx):
    rows, cols = mom.shape[1:]
    tok = act.shape[1]
    table = dct_table()
    dt = np.kron(np.eye(4, dtype=np.float32), table.T)
    tables = split_table(dt) + split_table(dt.T.copy())
    ct2 = np.concatenate([table.T, table.T], axis=1)
    vmem = pl.BlockSpec(memory_space=pltpu.VMEM)
    anyw = pl.BlockSpec(memory_space=pl.ANY)
    S = jax.ShapeDtypeStruct
    return pl.pallas_call(
        exchange_kernel,
        out_shape=(
            pltpu.VMEM((rows, cols), f32),
            pltpu.VMEM((EARLY * 256, cols), bf16),
            pltpu.VMEM((16, 7, 8, 128), f32),
            pltpu.VMEM((28, 6, 8, 128), f32),
        ),
        in_specs=[anyw] * 9,
        out_specs=(vmem, vmem, vmem, vmem),
        scratch_shapes=[
            pltpu.VMEM((tok, rows), bf16),
            pltpu.VMEM((tok, cols), bf16),
            pltpu.VMEM((cols, rows), f32),
            pltpu.VMEM(idx.shape, i32),
            pltpu.VMEM((42, 64, 128), f32),
            pltpu.VMEM((42, 128, 128), bf16),
            pltpu.VMEM((42, 128, 128), bf16),
            pltpu.VMEM((48, 128), f32),
        ]
        + [pltpu.VMEM((256, 256), bf16)] * 4
        + [
            pltpu.VMEM((64, 128), f32),
            pltpu.VMEM((256, cols), f32),
            pltpu.VMEM((256, cols), f32),
            pltpu.VMEM((4, 4, 8, 128), f32),
            pltpu.VMEM((4, 4, 8, 128), f32),
            pltpu.SemaphoreType.DMA((10,)),
            pltpu.SemaphoreType.DMA((11 + 4 * PIECES,)),
            pltpu.SemaphoreType.DMA((16, PIECES)),
            pltpu.SemaphoreType.DMA((16,)),
            pltpu.SemaphoreType.DMA((45,)),
            pltpu.SemaphoreType.DMA((16, 3)),
        ],
        compiler_params=pltpu.CompilerParams(collective_id=0, has_side_effects=True, vmem_limit_bytes=57 << 20),
        name="exchange",
    )(og, act, mom, idx, *tables, ct2)


def decode_chunks(first, last, vals, iuv, tables, update, s_bufs, v_bufs, ready=None, done=None):
    dth, dtl, dch, dcl = tables
    io = lax.broadcasted_iota(i32, (64, 128), 0).astype(f32).astype(bf16)
    io2 = lax.broadcasted_iota(i32, (128, 128), 0).astype(f32).astype(bf16)
    zero, zero2 = jnp.zeros((64, 128), bf16), jnp.zeros((128, 128), bf16)
    one2 = jnp.ones((128, 128), bf16)
    lane = lax.broadcasted_iota(i32, (1, 128), 1)

    def spread(row, n):
        return jnp.broadcast_to(row, (n, 128)).astype(bf16)

    def scatter(j):
        s_buf, v_buf = s_bufs[j % 2], v_bufs[j % 2]
        for g in range(4):
            got = [vals[4 * i + g, j] for i in range(4)]
            for ai in range(4):
                v_buf[ai, g] = jnp.concatenate([v[:, 32 * ai : 32 * ai + 32] for v in got], axis=1)
        for ai in range(4):
            for bp in range(3):
                left, right = [], []
                for bo in range(2):
                    b = 2 * bp + bo
                    for g in range(4):
                        hit = spread(iuv[4 * j + ai, b, g : g + 1, :], 64) == io
                        v = v_buf[ai, g, b : b + 1, :]
                        vh = v.astype(bf16).astype(f32)
                        left.append(
                            jnp.concatenate(
                                [jnp.where(hit, spread(vh, 64), zero), jnp.where(hit, spread(v - vh, 64), zero)], axis=0
                            )
                        )
                        at = spread(iuv[4 * j + ai, b, 4 + g : 5 + g, :] + 64.0 * bo, 128)
                        right.append(jnp.where(at == io2, one2, zero2))
                o = dot_t(jnp.concatenate(left, axis=1), jnp.concatenate(right, axis=1))
                s_buf[64 * ai : 64 * ai + 64, 128 * bp : 128 * bp + 128] = o[:64] + o[64:]

    def inverse(j):
        sh, sl = split(s_bufs[j % 2][...])
        t = jnp.concatenate(
            [
                dot3(sh[:, :256], sl[:, :256], dch[...], dcl[...]),
                dot3(sh[:, 256:], sl[:, 256:], dch[:128, :128], dcl[:128, :128]),
            ],
            axis=1,
        )
        th, tl = split(t)
        d = dot3(dth[...], dtl[...], th, tl)
        for ai in range(4):
            for bp in range(3):
                blk = d[64 * ai : 64 * ai + 64, 128 * bp : 128 * bp + 128]
                col = jnp.sum(blk * blk, axis=0, keepdims=True)
                lo = jnp.sum(jnp.where(lane < 64, col, 0.0), axis=1, keepdims=True)
                hi = jnp.sum(jnp.where(lane < 64, 0.0, col), axis=1, keepdims=True)
                q = jnp.where(lane < 64, lo, hi) * (1.0 / (SPAN * SPAN))
                r0 = j * 256 + 64 * ai
                update[r0 : r0 + 64, 128 * bp : 128 * bp + 128] = jnp.tanh(blk * lax.rsqrt(q + 1e-06)).astype(bf16)

    scatter(first)
    if ready is not None:
        ready()
    for j in range(first, last):
        if j + 1 < last:
            scatter(j + 1)
        inverse(j)
        if done is not None:
            done(j)


def decode_kernel(
    newmom_in, upd_in, vals, iuv, dth_hbm, dtl_hbm, dch_hbm, dcl_hbm, newmom, update,
    upd, dth, dtl, dch, dcl, s_a, s_b, v_a, v_b, sem,
):
    tables = (dth, dtl, dch, dcl)
    loads = [
        pltpu.make_async_copy(src, dst, sem.at[9 + i])
        for i, (src, dst) in enumerate(zip((dth_hbm, dtl_hbm, dch_hbm, dcl_hbm), tables))
    ]
    early = pl.ds(0, EARLY * 256)
    outs = [
        pltpu.make_async_copy(newmom_in, newmom.at[0], sem.at[7]),
        pltpu.make_async_copy(upd_in, update.at[early], sem.at[8]),
    ]
    for cp in loads + outs:
        cp.start()

    def ready():
        for cp in loads:
            cp.wait()

    def done(j):
        rows = pl.ds(j * 256, 256)
        cp = pltpu.make_async_copy(upd.at[rows], update.at[rows], sem.at[j])
        cp.start()
        outs.append(cp)

    decode_chunks(EARLY, 7, vals, iuv, tables, upd, (s_a, s_b), (v_a, v_b), ready, done)
    for cp in outs:
        cp.wait()


def decode(newmom, upd, vals, iuv):
    rows, cols = newmom.shape
    table = dct_table()
    dt = np.kron(np.eye(4, dtype=np.float32), table.T)
    tables = split_table(dt) + split_table(dt.T.copy())
    vmem = pl.BlockSpec(memory_space=pltpu.VMEM)
    anyw = pl.BlockSpec(memory_space=pl.ANY)
    S = jax.ShapeDtypeStruct
    return pl.pallas_call(
        decode_kernel,
        out_shape=(S((1, rows, cols), f32), S((rows, cols), bf16)),
        in_specs=[vmem] * 4 + [anyw] * 4,
        out_specs=(anyw, anyw),
        scratch_shapes=[pltpu.VMEM((rows, cols), bf16)]
        + [pltpu.VMEM((256, 256), bf16)] * 4
        + [
            pltpu.VMEM((256, cols), f32),
            pltpu.VMEM((256, cols), f32),
            pltpu.VMEM((4, 4, 8, 128), f32),
            pltpu.VMEM((4, 4, 8, 128), f32),
            pltpu.SemaphoreType.DMA((13,)),
        ],
        compiler_params=pltpu.CompilerParams(vmem_limit_bytes=57 << 20),
        name="decode",
    )(newmom, upd, vals, iuv, *tables)


def per_device(hidden_act, out_grads, momentum, coeff_index):
    newmom, upd, vals, iuv = exchange(out_grads, hidden_act, momentum, coeff_index.transpose(1, 2, 0, 3))
    held = [pltpu.with_memory_space_constraint(v, pltpu.VMEM) for v in (newmom, upd, vals, iuv)]
    return decode(*held)


def solution(mesh):
    placed = (
        P("rep", None, "tp"),
        P("rep", "tp", None),
        P("rep", "tp", None),
        P(None, "tp", None, None),
    )
    return jax.shard_map(
        per_device,
        mesh=mesh,
        in_specs=placed,
        out_specs=(P("rep", "tp", None), P("tp", None)),
        check_vma=False,
    )
```

```python
import functools

import jax
import jax.numpy as jnp
import ml_dtypes
import numpy as np
from jax import lax
from jax.experimental import pallas as pl
from jax.experimental.pallas import tpu as pltpu
from jax.sharding import PartitionSpec as P

SPAN = 64
DECAY = 0.9
PIECES = 4
EARLY = 3
MESH = pl.DeviceIdType.MESH
f32, bf16, i32 = jnp.float32, jnp.bfloat16, jnp.int32


def dct_table():
    n = np.arange(SPAN)
    u = np.arange(SPAN)[:, None]
    scale = np.where(u == 0, np.sqrt(1.0 / SPAN), np.sqrt(2.0 / SPAN))
    return (scale * np.cos(np.pi * (2 * n[None] + 1) * u / (2 * SPAN))).astype(np.float32)


def split_table(x):
    high = x.astype(ml_dtypes.bfloat16)
    low = (x - high.astype(np.float32)).astype(ml_dtypes.bfloat16)
    return high, low


def split(x):
    high = x.astype(bf16)
    return high, (x - high.astype(f32)).astype(bf16)


def dot(a, b):
    return jnp.dot(a, b, preferred_element_type=f32)


def dot_t(a, b):
    return lax.dot_general(a, b, (((1,), (1,)), ((), ())), preferred_element_type=f32)


def dot3(ah, al, bh, bl):
    return dot(ah, bh) + dot(al, bh) + dot(ah, bl)


def lane_gather(x, idx):
    return jnp.take_along_axis(x, idx, axis=1, mode="promise_in_bounds")


def exchange_kernel(
    og_hbm, act_hbm, mom_hbm, idx_hbm, dth_hbm, dtl_hbm, dch_hbm, dcl_hbm, ct2_hbm,
    mixed, upd, vals, iuv,
    act, og, gt, idx, cu, rh, rl, wrow, dth, dtl, dch, dcl, ct2, s_a, s_b, v_a, v_b,
    load_sem, og_send, og_recv, core_recv, v_send, v_recv,
):
    rep, tp = lax.axis_index("rep"), lax.axis_index("tp")
    y, zl = rep // 4, rep % 4
    zh, x, c = tp // 8, (tp // 2) % 4, tp % 2
    tok = og_hbm.shape[1]

    def tpid(zh_, x_, c_):
        return (zh_ * 4 + x_) * 2 + c_

    xs = [lax.rem(x + 1, 4), lax.rem(x + 3, 4), lax.rem(x + 2, 4)]
    x_peers = [tpid(zh, xx, c) for xx in xs]
    core_peer = tpid(zh, x, 1 - c)
    z_peer = tpid(1 - zh, x, c)
    z_reps = [y * 4 + lax.rem(zl + d, 4) for d in (1, 2, 3)]
    y_reps = [lax.rem(y + d, 4) * 4 + zl for d in (1, 3, 2)]
    far_reps = [lax.rem(y + d, 4) * 4 + lax.rem(zl + e, 4) for d in (1, 3, 2) for e in (1, 2, 3)]
    all_reps = z_reps + y_reps

    barrier = pltpu.get_barrier_semaphore()
    for t in x_peers + [core_peer, z_peer]:
        pl.semaphore_signal(barrier, inc=1, device_id=(rep, t), device_id_type=MESH)
    for r in all_reps:
        pl.semaphore_signal(barrier, inc=1, device_id=(r, tp), device_id_type=MESH)

    loads = []

    def load(src, dst):
        cp = pltpu.make_async_copy(src, dst, load_sem.at[len(loads)])
        cp.start()
        loads.append(cp)
        return cp

    def slot(t):
        return pl.ds(pl.multiple_of(t * tok, tok), tok)

    og_in = load(og_hbm.at[0], og.at[slot(tp)])
    idx_in = load(idx_hbm, idx)
    ct2_in = load(ct2_hbm, ct2)
    half = 4 * 2 * tok
    act_in = []
    for h in (zh, 1 - zh):
        rows = pl.ds(pl.multiple_of(h * half, half), half)
        act_in.append(load(act_hbm.at[0, rows], act.at[rows]))
    mom_in = load(mom_hbm.at[0], mixed)
    table_in = [load(dth_hbm, dth), load(dtl_hbm, dtl), load(dch_hbm, dch), load(dcl_hbm, dcl)]

    pl.semaphore_wait(barrier, 5 + len(all_reps))

    sends = []
    size = tok // PIECES

    def piece_copy(src_tp, dst_tp, p, k):
        rows = slot(src_tp) if p is None else pl.ds(pl.multiple_of(src_tp * tok + p * size, size), size)
        return pltpu.make_async_remote_copy(
            src_ref=og.at[rows],
            dst_ref=og.at[rows],
            send_sem=og_send.at[k],
            recv_sem=og_recv.at[src_tp, 0 if p is None else p],
            device_id=(rep, dst_tp),
            device_id_type=MESH,
        )

    def core_copy(src_tp, k):
        return pltpu.make_async_remote_copy(
            src_ref=og.at[slot(src_tp)],
            dst_ref=og.at[slot(src_tp)],
            send_sem=og_send.at[k],
            recv_sem=core_recv.at[src_tp],
            device_id=(rep, core_peer),
            device_id_type=MESH,
        )

    def send(src_tp, dst_tp, p):
        cp = piece_copy(src_tp, dst_tp, p, len(sends))
        cp.start()
        sends.append(cp)

    def send_core(src_tp):
        cp = core_copy(src_tp, len(sends))
        cp.start()
        sends.append(cp)

    def arrived(src_tp, p):
        piece_copy(src_tp, tp, p, 0).wait_recv()

    def arrived_core(src_tp):
        core_copy(src_tp, 0).wait_recv()

    og_in.wait()
    for p in range(PIECES):
        send(tp, z_peer, p)
    for t in x_peers:
        send(tp, t, None)
    send_core(tp)

    idx_in.wait()
    ct2_in.wait()

    def index_rows(a, _):
        for b in range(6):
            got = idx[a, b]
            row = jnp.concatenate([got[4 * i : 4 * i + 4] for i in range(4)], axis=1)
            iuv[a, b] = jnp.concatenate([row >> 6, row & 63], axis=0).astype(f32)
        return 0

    lax.fori_loop(0, 28, index_rows, 0)

    def own_tables(j, _):
        row_b = lax.broadcasted_iota(i32, (128, 128), 0) // 64
        lane = lax.broadcasted_iota(i32, (128, 128), 1)
        mine = row_b == (lane // 32) % 2
        for q in range(6):
            a2, bp = q // 3, q % 3
            row = jnp.concatenate(
                [idx[4 * j + 2 * a2 + ap, 2 * bp + b, pl.ds(rep, 1), :] for ap in range(2) for b in range(2)],
                axis=1,
            )
            k = j * 6 + q
            cu[k] = lane_gather(ct2[...], jnp.broadcast_to(row >> 6, (64, 128)))
            cv = lane_gather(ct2[...], jnp.broadcast_to(row & 63, (64, 128)))
            cvh, cvl = split(jnp.where(mine, jnp.concatenate([cv, cv], axis=0), 0.0))
            rh[k] = cvh
            rl[k] = cvl
        return 0

    lax.fori_loop(0, 7, own_tables, 0)
    for t in x_peers:
        arrived(t, None)
        send_core(t)
    for p in range(PIECES):
        arrived(z_peer, p)
        for t in x_peers:
            send(z_peer, t, p)
    send_core(z_peer)

    arrived_core(core_peer)
    for xx in xs:
        arrived_core(tpid(zh, xx, 1 - c))
    act_in[0].wait()

    def partial_grad(off, depth, first):
        off = pl.multiple_of(off, depth)
        bt = og[pl.ds(off, depth), :].T

        def body(j, _):
            cols = pl.ds(pl.multiple_of(j * 256, 256), 256)
            part = dot(bt, act[pl.ds(off, depth), cols])
            gt[:, cols] = part if first else gt[:, cols] + part
            return 0

        lax.fori_loop(0, 7, body, 0)

    partial_grad(zh * half, half, True)

    for xx in xs:
        t = tpid(1 - zh, xx, c)
        for p in range(PIECES):
            arrived(t, p)
        send_core(t)
    act_in[1].wait()

    def late_slots(core):
        return [slot(tpid(1 - zh, xx, core)) for xx in range(4)]

    mine = late_slots(c)
    bt1 = jnp.concatenate([og[r, :] for r in mine], axis=0).T

    def late_grad(j, _):
        cols = pl.ds(pl.multiple_of(j * 256, 256), 256)
        gt[:, cols] = gt[:, cols] + dot(bt1, jnp.concatenate([act[r, cols] for r in mine], axis=0))
        return 0

    lax.fori_loop(0, 7, late_grad, 0)

    mom_in.wait()
    for cp in table_in:
        cp.wait()
    arrived_core(tpid(1 - zh, x, 1 - c))
    for xx in xs:
        arrived_core(tpid(1 - zh, xx, 1 - c))

    theirs = late_slots(1 - c)
    bt2 = jnp.concatenate([og[r, :] for r in theirs], axis=0).T

    def forward(j):
        cols = slice(j * 256, j * 256 + 256)
        g = gt[:, cols] + dot(bt2, jnp.concatenate([act[r, cols] for r in theirs], axis=0))
        m = DECAY * mixed[cols, :] + g.T
        mixed[cols, :] = m
        mh, ml = split(m)
        lane = lax.broadcasted_iota(i32, (64, 128), 1)
        ws = []
        for q in range(6):
            a2, bp = q // 3, q % 3
            k = j * 6 + q
            rows = slice(128 * a2, 128 * a2 + 128)
            at = slice(128 * bp, 128 * bp + 128)
            t = dot(mh[rows, at], rh[k]) + dot(ml[rows, at], rh[k]) + dot(mh[rows, at], rl[k])
            got = jnp.where(lane < 64, t[:64], t[64:])
            w = jnp.sum(got * cu[j * 6 + q], axis=0, keepdims=True)
            wrow[j * 6 + q : j * 6 + q + 1, :] = w
            ws.append(w)
        rows = []
        for b in range(6):
            bp, bo = b // 2, 32 * (b % 2)
            rows.append(
                jnp.concatenate([ws[3 * a2 + bp][:, o + bo : o + bo + 32] for a2 in range(2) for o in (0, 64)], axis=1)
            )
        vals[rep, j] = jnp.concatenate(rows + [jnp.zeros((2, 128), f32)], axis=0)

    def vcopy(r, to, lo, n, si, ri):
        return pltpu.make_async_remote_copy(
            src_ref=vals.at[r, pl.ds(lo, n)],
            dst_ref=vals.at[r, pl.ds(lo, n)],
            send_sem=v_send.at[si],
            recv_sem=v_recv.at[r, ri],
            device_id=(to, tp),
            device_id_type=MESH,
        )

    groups = [(0, 4), (4, 2), (6, 1)]
    vsends = []

    def vsend(r, to, gi):
        cp = vcopy(r, to, *groups[gi], len(vsends), gi)
        cp.start()
        vsends.append(cp)

    def varrived(r, gi):
        vcopy(r, rep, *groups[gi], 0, gi).wait_recv()

    for j in range(4):
        forward(j)
    for r in z_reps + y_reps:
        vsend(rep, r, 0)
    for j in range(4, 6):
        forward(j)
    for r in z_reps + y_reps:
        vsend(rep, r, 1)
    for z in z_reps:
        varrived(z, 0)
        for r in y_reps:
            vsend(z, r, 0)
    forward(6)
    for r in all_reps:
        vsend(rep, r, 2)

    def keep(j):
        lane = lax.broadcasted_iota(i32, (64, 128), 1)
        for q in range(6):
            a2, bp = q // 3, q % 3
            k = j * 6 + q
            l = cu[k] * jnp.broadcast_to(wrow[k : k + 1, :], (64, 128))
            lh, ll = split(jnp.concatenate([jnp.where(lane < 64, l, 0.0), jnp.where(lane < 64, 0.0, l)], axis=0))
            kept = dot_t(lh, rh[k]) + dot_t(ll, rh[k]) + dot_t(lh, rl[k])
            rows = slice(j * 256 + a2 * 128, j * 256 + a2 * 128 + 128)
            cols = slice(bp * 128, bp * 128 + 128)
            mixed[rows, cols] = mixed[rows, cols] - kept

    for j in range(4):
        keep(j)
    for z in z_reps:
        varrived(z, 1)
        for r in y_reps:
            vsend(z, r, 1)
    for j in range(4, 7):
        keep(j)
    for z in z_reps:
        varrived(z, 2)
        for r in y_reps:
            vsend(z, r, 2)

    for r in y_reps + far_reps:
        varrived(r, 0)
    if EARLY:
        decode_chunks(0, EARLY, vals, iuv, (dth, dtl, dch, dcl), upd, (s_a, s_b), (v_a, v_b))
    for r in y_reps + far_reps:
        varrived(r, 1)
    for r in y_reps + far_reps:
        varrived(r, 2)
    for cp in sends + vsends:
        cp.wait_send()


def exchange(og, act, mom, idx):
    rows, cols = mom.shape[1:]
    tok = act.shape[1]
    table = dct_table()
    dt = np.kron(np.eye(4, dtype=np.float32), table.T)
    tables = split_table(dt) + split_table(dt.T.copy())
    ct2 = np.concatenate([table.T, table.T], axis=1)
    vmem = pl.BlockSpec(memory_space=pltpu.VMEM)
    anyw = pl.BlockSpec(memory_space=pl.ANY)
    S = jax.ShapeDtypeStruct
    return pl.pallas_call(
        exchange_kernel,
        out_shape=(
            pltpu.VMEM((rows, cols), f32),
            pltpu.VMEM((EARLY * 256, cols), bf16),
            pltpu.VMEM((16, 7, 8, 128), f32),
            pltpu.VMEM((28, 6, 8, 128), f32),
        ),
        in_specs=[anyw] * 9,
        out_specs=(vmem, vmem, vmem, vmem),
        scratch_shapes=[
            pltpu.VMEM((tok, rows), bf16),
            pltpu.VMEM((tok, cols), bf16),
            pltpu.VMEM((cols, rows), f32),
            pltpu.VMEM(idx.shape, i32),
            pltpu.VMEM((42, 64, 128), f32),
            pltpu.VMEM((42, 128, 128), bf16),
            pltpu.VMEM((42, 128, 128), bf16),
            pltpu.VMEM((48, 128), f32),
        ]
        + [pltpu.VMEM((256, 256), bf16)] * 4
        + [
            pltpu.VMEM((64, 128), f32),
            pltpu.VMEM((256, cols), f32),
            pltpu.VMEM((256, cols), f32),
            pltpu.VMEM((4, 4, 8, 128), f32),
            pltpu.VMEM((4, 4, 8, 128), f32),
            pltpu.SemaphoreType.DMA((10,)),
            pltpu.SemaphoreType.DMA((11 + 4 * PIECES,)),
            pltpu.SemaphoreType.DMA((16, PIECES)),
            pltpu.SemaphoreType.DMA((16,)),
            pltpu.SemaphoreType.DMA((45,)),
            pltpu.SemaphoreType.DMA((16, 3)),
        ],
        compiler_params=pltpu.CompilerParams(collective_id=0, has_side_effects=True, vmem_limit_bytes=57 << 20),
        name="exchange",
    )(og, act, mom, idx, *tables, ct2)


def decode_chunks(first, last, vals, iuv, tables, update, s_bufs, v_bufs, ready=None, done=None):
    dth, dtl, dch, dcl = tables
    io = lax.broadcasted_iota(i32, (64, 128), 0).astype(f32).astype(bf16)
    io2 = lax.broadcasted_iota(i32, (128, 128), 0).astype(f32).astype(bf16)
    zero, zero2 = jnp.zeros((64, 128), bf16), jnp.zeros((128, 128), bf16)
    one2 = jnp.ones((128, 128), bf16)
    lane = lax.broadcasted_iota(i32, (1, 128), 1)

    def spread(row, n):
        return jnp.broadcast_to(row, (n, 128)).astype(bf16)

    def scatter(j):
        s_buf, v_buf = s_bufs[j % 2], v_bufs[j % 2]
        for g in range(4):
            got = [vals[4 * i + g, j] for i in range(4)]
            for ai in range(4):
                v_buf[ai, g] = jnp.concatenate([v[:, 32 * ai : 32 * ai + 32] for v in got], axis=1)
        for ai in range(4):
            for bp in range(3):
                left, right = [], []
                for bo in range(2):
                    b = 2 * bp + bo
                    for g in range(4):
                        hit = spread(iuv[4 * j + ai, b, g : g + 1, :], 64) == io
                        v = v_buf[ai, g, b : b + 1, :]
                        vh = v.astype(bf16).astype(f32)
                        left.append(
                            jnp.concatenate(
                                [jnp.where(hit, spread(vh, 64), zero), jnp.where(hit, spread(v - vh, 64), zero)], axis=0
                            )
                        )
                        at = spread(iuv[4 * j + ai, b, 4 + g : 5 + g, :] + 64.0 * bo, 128)
                        right.append(jnp.where(at == io2, one2, zero2))
                o = dot_t(jnp.concatenate(left, axis=1), jnp.concatenate(right, axis=1))
                s_buf[64 * ai : 64 * ai + 64, 128 * bp : 128 * bp + 128] = o[:64] + o[64:]

    def inverse(j):
        sh, sl = split(s_bufs[j % 2][...])
        t = jnp.concatenate(
            [
                dot3(sh[:, :256], sl[:, :256], dch[...], dcl[...]),
                dot3(sh[:, 256:], sl[:, 256:], dch[:128, :128], dcl[:128, :128]),
            ],
            axis=1,
        )
        th, tl = split(t)
        d = dot3(dth[...], dtl[...], th, tl)
        for ai in range(4):
            for bp in range(3):
                blk = d[64 * ai : 64 * ai + 64, 128 * bp : 128 * bp + 128]
                col = jnp.sum(blk * blk, axis=0, keepdims=True)
                lo = jnp.sum(jnp.where(lane < 64, col, 0.0), axis=1, keepdims=True)
                hi = jnp.sum(jnp.where(lane < 64, 0.0, col), axis=1, keepdims=True)
                q = jnp.where(lane < 64, lo, hi) * (1.0 / (SPAN * SPAN))
                r0 = j * 256 + 64 * ai
                update[r0 : r0 + 64, 128 * bp : 128 * bp + 128] = jnp.tanh(blk * lax.rsqrt(q + 1e-06)).astype(bf16)

    scatter(first)
    if ready is not None:
        ready()
    for j in range(first, last):
        if j + 1 < last:
            scatter(j + 1)
        inverse(j)
        if done is not None:
            done(j)


def decode_kernel(
    newmom_in, upd_in, vals, iuv, dth_hbm, dtl_hbm, dch_hbm, dcl_hbm, newmom, update,
    upd, dth, dtl, dch, dcl, s_a, s_b, v_a, v_b, sem,
):
    tables = (dth, dtl, dch, dcl)
    loads = [
        pltpu.make_async_copy(src, dst, sem.at[9 + i])
        for i, (src, dst) in enumerate(zip((dth_hbm, dtl_hbm, dch_hbm, dcl_hbm), tables))
    ]
    early = pl.ds(0, EARLY * 256)
    outs = [
        pltpu.make_async_copy(newmom_in, newmom.at[0], sem.at[7]),
        pltpu.make_async_copy(upd_in, update.at[early], sem.at[8]),
    ]
    for cp in loads + outs:
        cp.start()

    def ready():
        for cp in loads:
            cp.wait()

    def done(j):
        rows = pl.ds(j * 256, 256)
        cp = pltpu.make_async_copy(upd.at[rows], update.at[rows], sem.at[j])
        cp.start()
        outs.append(cp)

    decode_chunks(EARLY, 7, vals, iuv, tables, upd, (s_a, s_b), (v_a, v_b), ready, done)
    for cp in outs:
        cp.wait()


def decode(newmom, upd, vals, iuv):
    rows, cols = newmom.shape
    table = dct_table()
    dt = np.kron(np.eye(4, dtype=np.float32), table.T)
    tables = split_table(dt) + split_table(dt.T.copy())
    vmem = pl.BlockSpec(memory_space=pltpu.VMEM)
    anyw = pl.BlockSpec(memory_space=pl.ANY)
    S = jax.ShapeDtypeStruct
    return pl.pallas_call(
        decode_kernel,
        out_shape=(S((1, rows, cols), f32), S((rows, cols), bf16)),
        in_specs=[vmem] * 4 + [anyw] * 4,
        out_specs=(anyw, anyw),
        scratch_shapes=[pltpu.VMEM((rows, cols), bf16)]
        + [pltpu.VMEM((256, 256), bf16)] * 4
        + [
            pltpu.VMEM((256, cols), f32),
            pltpu.VMEM((256, cols), f32),
            pltpu.VMEM((4, 4, 8, 128), f32),
            pltpu.VMEM((4, 4, 8, 128), f32),
            pltpu.SemaphoreType.DMA((13,)),
        ],
        compiler_params=pltpu.CompilerParams(vmem_limit_bytes=57 << 20),
        name="decode",
    )(newmom, upd, vals, iuv, *tables)


def per_device(hidden_act, out_grads, momentum, coeff_index):
    newmom, upd, vals, iuv = exchange(out_grads, hidden_act, momentum, coeff_index.transpose(1, 2, 0, 3))
    held = [pltpu.with_memory_space_constraint(v, pltpu.VMEM) for v in (newmom, upd, vals, iuv)]
    return decode(*held)


def solution(mesh):
    placed = (
        P("rep", None, "tp"),
        P("rep", "tp", None),
        P("rep", "tp", None),
        P(None, "tp", None, None),
    )
    return jax.shard_map(
        per_device,
        mesh=mesh,
        in_specs=placed,
        out_specs=(P("rep", "tp", None), P("tp", None)),
        check_vma=False,
    )
```
